128 devices in a mesh: dp: 16 (over z, x_lo, core), mp: 8 (over x_hi, y).
Axes of the slice: x: 4 (x_hi: 2, x_lo: 2; x = x_hi * 2 + x_lo), y: 4, z: 4, core: 2. Of those that a mesh axis runs over, the one named last changes fastest.
Arguments:
- old_store: bfloat16 [4096, 4096], P('mp', 'dp'), may hold values from -0.09375 to 0.09375
- block_map: int32 [32], replicated, may hold values from 0 to 31, each once
- expand_in: bfloat16 [8192, 4096], P('mp', 'dp'), may hold values from -0.0625 to 0.0625
- expand_out: bfloat16 [8192, 4096], P('dp'), may hold values from -0.09375 to 0.09375
- attn: bfloat16 [4096, 8192], P('dp', 'mp'), may hold values from -6 to 6
- residual: bfloat16 [4096, 8192], P('dp', 'mp'), may hold values from -6 to 6
Outputs:
- stream: bfloat16 [4096, 8192], P('dp', 'mp')
The draws below stay inside these ranges and needn't reach their ends.
Inputs may be any that keep to these rules, and one draw needn't show every extreme that they name: `block_map`: a permutation: every row block of the old weight is held by exactly one stored block.
All inputs are finite; a program needn't handle non-finite values.
Results may differ from the reference program's by a relative error of at most 0.023.
Values may be sent and summed in bfloat16 or wider, within the bound.
A program may use at most 128 MiB of HBM per device.

```python
import jax
import jax.numpy as jnp
from jax import lax

D_OLD = 4096
D_NEW = 8192
BLOCK = 128
NBLOCKS = 32
TOKENS = 4096
N_DP = 16
N_MP = 8


def steps_of(rng, shape, split, smallest, high):
    def one(position, blocks):
        steps = jax.random.uniform(jax.random.fold_in(jax.random.fold_in(rng, 6), position), (blocks,), jnp.float32, smallest / len(split), high / len(split))
        return jnp.repeat(jnp.exp(steps), shape[position] // blocks).reshape((-1,) + (1,) * (len(shape) - position - 1))

    loudness = one(*split[0])
    for cut in split[1:]:
        loudness = loudness * one(*cut)
    return loudness


def centred(stream_key, dims, spread, reach, split=(), kind=jnp.bfloat16):
    entries = jax.random.normal(stream_key, dims, jnp.float32) * spread
    if len(split) > 0:
        entries = steps_of(stream_key, dims, split, -0.22, 0.18) * entries
    return jnp.clip(entries, min=-reach, max=reach).astype(kind)


def setup_inputs(seed: int = 0) -> dict:
    splits = jax.random.split(jax.random.key(seed), 7)
    old_store = centred(splits[0], (D_OLD, D_OLD), D_OLD ** -0.5, 0.09375, ((0, 8), (1, 16)))
    block_map = jax.random.permutation(splits[1], NBLOCKS).astype(jnp.int32)
    expand_in = centred(splits[2], (D_NEW, D_OLD), D_NEW ** -0.5, 0.0625, ((0, 8), (1, 16)))
    expand_out = centred(splits[3], (D_NEW, D_OLD), D_OLD ** -0.5, 0.09375, ((0, 16),))
    attn = centred(splits[4], (TOKENS, D_NEW), 1.0, 6.0, ((0, 16), (1, 8)))
    residual = centred(splits[5], (TOKENS, D_NEW), 1.0, 6.0, ((0, 16), (1, 8)))
    return {"old_store": old_store, "block_map": block_map, "expand_in": expand_in, "expand_out": expand_out, "attn": attn, "residual": residual}


def contract_last(left_side, right_side):
    return lax.dot_general(left_side, right_side, (((1,), (1,)), ((), ())), preferred_element_type=jnp.float32)


def reference(old_store, block_map, expand_in, expand_out, attn, residual):
    block_count = D_OLD // BLOCK
    slot_ids = jnp.arange(block_count, dtype=jnp.int32)
    source = jnp.sum(jnp.where(block_map[None, :] == slot_ids[:, None], slot_ids[None, :], 0), axis=1).astype(jnp.int32)
    restored = jnp.take(old_store.reshape(block_count, BLOCK, D_OLD), source, axis=0).reshape(D_OLD, D_OLD)
    col_width = D_OLD // N_DP
    right = jnp.zeros((D_OLD, D_NEW), jnp.float32)
    for member in range(N_DP):
        columns = restored[:, member * col_width:(member + 1) * col_width]
        in_rows = expand_in[:, member * col_width:(member + 1) * col_width]
        partial_value = lax.optimization_barrier(contract_last(columns, in_rows).astype(jnp.bfloat16))
        right = right + partial_value.astype(jnp.float32)
    right = right.astype(jnp.bfloat16)
    grown = jnp.dot(expand_out, right, preferred_element_type=jnp.float32).astype(jnp.bfloat16)
    out_width = D_NEW // N_MP
    stream = residual.astype(jnp.float32)
    for member in range(N_MP):
        features = attn[:, member * out_width:(member + 1) * out_width]
        weights = grown[:, member * out_width:(member + 1) * out_width]
        partial_value = lax.optimization_barrier(contract_last(features, weights).astype(jnp.bfloat16))
        stream = stream + partial_value.astype(jnp.float32)
    return stream.astype(jnp.bfloat16)
```

```python
import jax
import jax.numpy as jnp
from jax import lax
from jax.experimental import pallas as pl
from jax.experimental.pallas import tpu as pltpu
from jax.sharding import PartitionSpec as P

MESH = pl.DeviceIdType.MESH
BLOCK = 128
NCH = 2
F32 = jnp.float32
BF16 = jnp.bfloat16


def place(z, xl, c, xh, y):
    return {"dp": z * 4 + xl * 2 + c, "mp": xh * 4 + y}


def dot_nt(a, b):
    return lax.dot_general(a, b, (((1,), (1,)), ((), ())), preferred_element_type=F32)


def chain_kernel(
    map_ref, store_ref, ein_ref, eout_ref, attn_ref, out_ref,
    attn_g, ein_g, s_g, eo_raw, eo, p1, r1, ysum, xs, xr, a1g, p2, r2, a2g, ob,
    loc_sem, ein_ss, ein_rs, s_ss, s_rs, at_ss, at_rs, eo_ss, eo_rs, r1_ss, r1_rs, x_ss, x_rs,
    a1_ss, a1_rs, r2_ss, r2_rs, a2_ss, a2_rs, out_ss, out_rs,
):
    d = lax.axis_index("dp")
    m = lax.axis_index("mp")
    z, xl, c = d // 4, (d // 2) % 2, d % 2
    xh, y = m // 4, m % 4
    p = z * 2 + xl
    q0 = xl * 2 + c
    ox, oc, oh = 1 - xl, 1 - c, 1 - xh
    rows = attn_ref.shape[0] // NCH
    ry, rx = rows // 4, rows // 8
    sent = []

    def remote(src, dst, ss, rs, target):
        return pltpu.make_async_remote_copy(
            src_ref=src, dst_ref=dst, send_sem=ss, recv_sem=rs, device_id=target, device_id_type=MESH
        )

    def send(src, dst, ss, rs, target):
        copy = remote(src, dst, ss, rs, target)
        copy.start()
        sent.append(copy)

    def arrived(dst, ss, rs):
        remote(dst, dst, ss, rs, place(z, xl, oc, xh, y)).wait_recv()

    def zk(k):
        return lax.rem(z + k, 4)

    def yk(k):
        return lax.rem(y + k, 4)

    local = [
        pltpu.make_async_copy(attn_ref, attn_g.at[z], loc_sem.at[0]),
        pltpu.make_async_copy(ein_ref, ein_g.at[q0], loc_sem.at[1]),
        pltpu.make_async_copy(store_ref, s_g.at[q0, xh], loc_sem.at[2]),
    ]
    for copy in local:
        copy.start()

    @pl.loop(0, 32)
    def _(t):
        cols = pl.ds(pl.multiple_of(t * BLOCK, BLOCK), BLOCK)
        pltpu.make_async_copy(eout_ref.at[:, cols], eo_raw.at[t], loc_sem.at[3]).start()

    barrier = pltpu.get_barrier_semaphore()

    def greet(target):
        pl.semaphore_signal(barrier, inc=1, device_id=target, device_id_type=MESH)

    greet(place(z, xl, oc, xh, y))
    greet(place(z, ox, c, xh, y))
    greet(place(z, xl, c, oh, y))
    greet(place(z, ox, c, oh, y))
    for k in range(1, 4):
        greet(place(z, xl, c, xh, yk(k)))
        greet(place(zk(k), xl, c, xh, y))
        greet(place(zk(k), ox, c, xh, y))
        for l in range(1, 4):
            greet(place(zk(k), xl, c, xh, yk(l)))
    greeted = 4 + 3 * 6
    self_out = p == m
    for ms in range(8):
        @pl.when(jnp.logical_not(jnp.logical_and(self_out, m == ms)))
        def _():
            greet(place(m // 2, m % 2, c, ms // 4, ms % 4))
    pl.semaphore_wait(barrier, greeted + 8 - jnp.where(self_out, 1, 0))

    send(ein_ref, ein_g.at[q0], ein_ss.at[0], ein_rs.at[q0], place(z, xl, oc, xh, y))
    send(ein_ref, ein_g.at[q0], ein_ss.at[1], ein_rs.at[q0], place(z, ox, c, xh, y))
    for j in range(NCH):
        part = pl.ds(j * rows, rows)
        for k in (1, 3, 2):
            send(attn_ref.at[part], attn_g.at[z, part], at_ss.at[j, k], at_rs.at[j, z],
                 place(zk(k), xl, c, xh, y))
    mine = s_g.at[q0, xh]
    send(store_ref, mine, s_ss.at[0], s_rs.at[q0, xh], place(z, ox, c, xh, y))
    send(store_ref, mine, s_ss.at[1], s_rs.at[q0, xh], place(z, xl, c, oh, y))
    send(store_ref, mine, s_ss.at[2], s_rs.at[q0, xh], place(z, ox, c, oh, y))
    send(store_ref, mine, s_ss.at[3], s_rs.at[q0, xh], place(z, xl, oc, xh, y))

    pltpu.make_async_copy(eo_raw, eo_raw, loc_sem.at[3]).wait()

    @pl.loop(0, 32)
    def _(t):
        zs, ys, b = t // 8, (t // 2) % 4, t % 2
        s = ((zs // 2) * 4 + ys) * 4 + (zs % 2) * 2 + b
        eo[c, :, pl.ds(pl.multiple_of(t * BLOCK, BLOCK), BLOCK)] = eo_raw[map_ref[s]]

    send(eo.at[c], eo.at[c], eo_ss, eo_rs, place(z, xl, oc, xh, y))

    local[0].wait()
    local[1].wait()

    def multiply_in(j, q):
        lhs = attn_g[:, pl.ds(j * rows, rows), :].reshape(4 * rows, -1)
        res = jnp.dot(lhs, ein_g[q], preferred_element_type=F32).astype(BF16)
        res = res.reshape(4, 4, ry, 256)
        cols = pl.ds(pl.multiple_of(q * 256, 256), 256)
        for yt in range(4):
            p1[j, yt, :, :, cols] = res[:, yt]

    def half_cols(h):
        return pl.ds(pl.multiple_of(h * 512, 512), 512)

    def send_partials(j, hr):
        h = xl if hr == 0 else ox
        for k in (1, 3, 2):
            send(p1.at[j, yk(k), :, :, half_cols(h)], r1.at[j, hr, 3 - k], r1_ss.at[j, hr, k],
                 r1_rs.at[j, hr, 3 - k], place(z, xl, c, xh, yk(k)))

    for j in range(NCH):
        for k in (1, 3, 2):
            arrived(attn_g.at[zk(k), pl.ds(j * rows, rows)], at_ss.at[j, k], at_rs.at[j, zk(k)])
        for hr in range(2):
            qa = (xl if hr == 0 else ox) * 2 + c
            qb = (xl if hr == 0 else ox) * 2 + oc
            if j == 0:
                if hr == 1:
                    arrived(ein_g.at[qa], ein_ss.at[1], ein_rs.at[qa])
                    send(ein_g.at[qa], ein_g.at[qa], ein_ss.at[2], ein_rs.at[qa], place(z, xl, oc, xh, y))
            multiply_in(j, qa)
            if j == 0:
                arrived(ein_g.at[qb], ein_ss.at[0], ein_rs.at[qb])
            multiply_in(j, qb)
            send_partials(j, hr)

    local[2].wait()
    for i, (xls, xhs) in enumerate(((ox, xh), (xl, oh), (ox, oh))):
        qs = xls * 2 + c
        arrived(s_g.at[qs, xhs], s_ss.at[0], s_rs.at[qs, xhs])
        send(s_g.at[qs, xhs], s_g.at[qs, xhs], s_ss.at[4 + i], s_rs.at[qs, xhs], place(z, xl, oc, xh, y))

    def reduce_y(j, hr):
        h = xl if hr == 0 else ox
        cols = half_cols(h)
        for k in range(3):
            arrived(r1.at[j, hr, k], r1_ss.at[j, hr, 1], r1_rs.at[j, hr, k])

        @pl.loop(0, 4)
        def _(zs):
            total = p1[j, y, zs, :, cols].astype(F32)
            for k in range(3):
                total = total + r1[j, hr, k, zs].astype(F32)
            low, high = total[:rx], total[rx:]
            ysum[j, hr, zs] = jnp.where(xh == 0, low, high)
            xs[j, hr, zs] = jnp.where(xh == 0, high, low).astype(BF16)

        send(xs.at[j, hr], xr.at[j, hr], x_ss.at[j, hr], x_rs.at[j, hr], place(z, xl, c, oh, y))

    def reduce_x(j, hr):
        h = xl if hr == 0 else ox
        arrived(xr.at[j, hr], x_ss.at[j, hr], x_rs.at[j, hr])
        total = ysum[j, hr] + xr[j, hr].astype(F32)
        a1g[j, h, y] = total.astype(BF16).reshape(4 * rx, 512)
        for k in (1, 3, 2):
            send(a1g.at[j, h, y], a1g.at[j, h, y], a1_ss.at[j, hr, k], a1_rs.at[j, hr, y],
                 place(z, xl, c, xh, yk(k)))

    def multiply_store(j):
        for hr in range(2):
            h = xl if hr == 0 else ox
            for k in range(1, 4):
                arrived(a1g.at[j, h, yk(k)], a1_ss.at[j, hr, k], a1_rs.at[j, hr, yk(k)])

        @pl.loop(0, 4)
        def _(zt):
            total = jnp.zeros((16 * rx, 256), F32)
            for q in range(4):
                lhs = a1g[j, q // 2, :, :, (q % 2) * 256:(q % 2 + 1) * 256].reshape(16 * rx, 256)
                rhs = s_g[q, zt // 2, pl.ds(pl.multiple_of((zt % 2) * 256, 256), 256), :]
                total = total + dot_nt(lhs, rhs)
            p2[j, zt] = total.astype(BF16).reshape(4, 4 * rx, 256)

        for k in range(4):
            for l in range(4):
                if k or l:
                    send(p2.at[j, zk(k), yk(l)], r2.at[j, z, y], r2_ss.at[j, k, l], r2_rs.at[j, z, y],
                         place(zk(k), xl, c, xh, yk(l)))
        r2[j, z, y] = p2[j, z, y]

    def reduce_z(j):
        for k in range(4):
            for l in range(4):
                if k or l:
                    arrived(r2.at[j, zk(k), yk(l)], r2_ss.at[j, k, l], r2_rs.at[j, zk(k), yk(l)])
        for ys in range(4):
            total = r2[j, 0, ys].astype(F32)
            for zs in range(1, 4):
                total = total + r2[j, zs, ys].astype(F32)
            a2g[j, xl, z, :, ys * 256:(ys + 1) * 256] = total.astype(BF16)
        for k in range(4):
            for l in range(2):
                if k or l:
                    send(a2g.at[j, xl, z], a2g.at[j, xl, z], a2_ss.at[j, l, k], a2_rs.at[j, xl, z],
                         place(zk(k), ox if l else xl, c, xh, y))

    def multiply_out(j):
        for k in range(4):
            for l in range(2):
                if k or l:
                    xs_ = ox if l else xl
                    arrived(a2g.at[j, xs_, zk(k)], a2_ss.at[j, l, k], a2_rs.at[j, xs_, zk(k)])

        @pl.loop(0, 4)
        def _(t):
            total = jnp.zeros((8 * rx, 256), F32)
            part = pl.ds(pl.multiple_of((t % 2) * 256, 256), 256)
            for zs in range(4):
                lhs = a2g[j, :, zs].reshape(8 * rx, 1024)
                total = total + dot_nt(lhs, eo[t // 2, part, zs * 1024:(zs + 1) * 1024])
            ob[j, :, :, :, pl.ds(pl.multiple_of(t * 256, 256), 256)] = total.astype(BF16).reshape(2, 4, rx, 256)

        for xt in range(2):
            for zt in range(4):
                dst = out_ref.at[pl.ds(pl.multiple_of(j * rows + y * ry + xh * rx, rx), rx)]
                src = ob.at[j, xt, zt]
                here = jnp.logical_and(self_out, jnp.logical_and(xl == xt, z == zt))

                @pl.when(here)
                def _():
                    pltpu.make_async_copy(src, dst, out_rs.at[j, m]).start()

                @pl.when(jnp.logical_not(here))
                def _():
                    remote(src, dst, out_ss.at[j, xt, zt], out_rs.at[j, m],
                           place(zt, xt, c, p // 4, p % 4)).start()

    def finish(j):
        for ms in range(8):
            dst = out_ref.at[pl.ds(j * rows + (ms % 4) * ry + (ms // 4) * rx, rx)]
            arrived(dst, out_ss.at[j, 0, 0], out_rs.at[j, ms])
        for xt in range(2):
            for zt in range(4):
                here = jnp.logical_and(self_out, jnp.logical_and(xl == xt, z == zt))

                @pl.when(jnp.logical_not(here))
                def _():
                    src = ob.at[j, xt, zt]
                    remote(src, src, out_ss.at[j, xt, zt], out_rs.at[j, m],
                           place(z, xl, oc, xh, y)).wait_send()

    for j in range(NCH):
        for hr in range(2):
            reduce_y(j, hr)
            reduce_x(j, hr)
        if j == 0:
            for xls in range(2):
                for xhs in range(2):
                    qs = xls * 2 + oc
                    arrived(s_g.at[qs, xhs], s_ss.at[0], s_rs.at[qs, xhs])
    for j in range(NCH):
        multiply_store(j)
    for j in range(NCH):
        reduce_z(j)
    arrived(eo.at[oc], eo_ss, eo_rs)
    for j in range(NCH):
        multiply_out(j)
    for j in range(NCH):
        finish(j)
    for copy in sent:
        copy.wait_send()


def shards(old_store, block_map, expand_in, expand_out, attn, residual):
    tokens, width = attn.shape
    rows = tokens // NCH
    ry, rx = rows // 4, rows // 8
    dma = pltpu.SemaphoreType.DMA
    hbm = pl.BlockSpec(memory_space=pl.ANY)
    products = pl.pallas_call(
        chain_kernel,
        out_shape=jax.ShapeDtypeStruct((tokens, width), BF16),
        in_specs=[pl.BlockSpec(memory_space=pltpu.SMEM), hbm, hbm, hbm, hbm],
        out_specs=hbm,
        scratch_shapes=[
            pltpu.VMEM((4, tokens, width), BF16),
            pltpu.VMEM((4, width, 256), BF16),
            pltpu.VMEM((4, 2, 512, 256), BF16),
            pltpu.VMEM((32, 512, BLOCK), BF16),
            pltpu.VMEM((2, 512, 4096), BF16),
            pltpu.VMEM((NCH, 4, 4, ry, 1024), BF16),
            pltpu.VMEM((NCH, 2, 3, 4, ry, 512), BF16),
            pltpu.VMEM((NCH, 2, 4, rx, 512), F32),
            pltpu.VMEM((NCH, 2, 4, rx, 512), BF16),
            pltpu.VMEM((NCH, 2, 4, rx, 512), BF16),
            pltpu.VMEM((NCH, 2, 4, 4 * rx, 512), BF16),
            pltpu.VMEM((NCH, 4, 4, 4 * rx, 256), BF16),
            pltpu.VMEM((NCH, 4, 4, 4 * rx, 256), BF16),
            pltpu.VMEM((NCH, 2, 4, 4 * rx, 1024), BF16),
            pltpu.VMEM((NCH, 2, 4, rx, 1024), BF16),
            dma((4,)), dma((3,)), dma((4,)), dma((7,)), dma((4, 2)),
            dma((NCH, 4)), dma((NCH, 4)), dma, dma,
            dma((NCH, 2, 4)), dma((NCH, 2, 3)), dma((NCH, 2)), dma((NCH, 2)),
            dma((NCH, 2, 4)), dma((NCH, 2, 4)), dma((NCH, 4, 4)), dma((NCH, 4, 4)),
            dma((NCH, 2, 4)), dma((NCH, 2, 4)), dma((NCH, 2, 4)), dma((NCH, 8)),
        ],
        compiler_params=pltpu.CompilerParams(
            collective_id=0, has_side_effects=True, vmem_limit_bytes=56 * 2**20
        ),
        name="chain",
    )(block_map, old_store, expand_in, expand_out, attn)
    return (products.astype(F32) + residual.astype(F32)).astype(BF16)


def solution(mesh):
    placed = (P("mp", "dp"), P(), P("mp", "dp"), P("dp", None), P("dp", "mp"), P("dp", "mp"))
    return jax.shard_map(
        shards, mesh=mesh, in_specs=placed, out_specs=P("dp", "mp"), check_vma=False
    )
```

```python
import jax
import jax.numpy as jnp
from jax import lax
from jax.experimental import pallas as pl
from jax.experimental.pallas import tpu as pltpu
from jax.sharding import PartitionSpec as P

MESH = pl.DeviceIdType.MESH
BLOCK = 128
NCH = 2
F32 = jnp.float32
BF16 = jnp.bfloat16


def place(z, xl, c, xh, y):
    return {"dp": z * 4 + xl * 2 + c, "mp": xh * 4 + y}


def dot_nt(a, b):
    return lax.dot_general(a, b, (((1,), (1,)), ((), ())), preferred_element_type=F32)


def chain_kernel(
    map_ref, store_ref, ein_ref, eout_ref, attn_ref, out_ref,
    attn_g, ein_g, s_g, eo_raw, eo, p1, r1, ysum, xs, xr, a1g, p2, r2, a2g, ob, ow,
    loc_sem, ein_ss, ein_rs, s_ss, s_rs, at_ss, at_rs, eo_ss, eo_rs, r1_ss, r1_rs, x_ss, x_rs,
    a1_ss, a1_rs, r2_ss, r2_rs, a2_ss, a2_rs, diag_ss, diag_rs, ow_ss, ow_rs, out_ss, out_rs,
):
    d = lax.axis_index("dp")
    m = lax.axis_index("mp")
    z, xl, c = d // 4, (d // 2) % 2, d % 2
    xh, y = m // 4, m % 4
    q0 = xl * 2 + c
    ox, oc, oh = 1 - xl, 1 - c, 1 - xh
    rows = attn_ref.shape[0] // NCH
    ry, rx = rows // 4, rows // 8
    sent = []

    def remote(src, dst, ss, rs, target):
        return pltpu.make_async_remote_copy(
            src_ref=src, dst_ref=dst, send_sem=ss, recv_sem=rs, device_id=target, device_id_type=MESH
        )

    def send(src, dst, ss, rs, target):
        copy = remote(src, dst, ss, rs, target)
        copy.start()
        sent.append(copy)

    def arrived(dst, ss, rs):
        remote(dst, dst, ss, rs, place(z, xl, oc, xh, y)).wait_recv()

    def zk(k):
        return lax.rem(z + k, 4)

    def yk(k):
        return lax.rem(y + k, 4)

    local = [
        pltpu.make_async_copy(attn_ref, attn_g.at[z], loc_sem.at[0]),
        pltpu.make_async_copy(ein_ref, ein_g.at[q0], loc_sem.at[1]),
        pltpu.make_async_copy(store_ref, s_g.at[q0, xh], loc_sem.at[2]),
    ]
    for copy in local:
        copy.start()

    @pl.loop(0, 32)
    def _(t):
        cols = pl.ds(pl.multiple_of(t * BLOCK, BLOCK), BLOCK)
        pltpu.make_async_copy(eout_ref.at[:, cols], eo_raw.at[t], loc_sem.at[3]).start()

    barrier = pltpu.get_barrier_semaphore()

    def greet(target):
        pl.semaphore_signal(barrier, inc=1, device_id=target, device_id_type=MESH)

    greet(place(z, xl, oc, xh, y))
    greet(place(z, ox, c, xh, y))
    greet(place(z, xl, c, oh, y))
    greet(place(z, ox, c, oh, y))
    for k in range(1, 4):
        greet(place(z, xl, c, xh, yk(k)))
        greet(place(zk(k), xl, c, xh, y))
        for l in range(1, 4):
            greet(place(zk(k), xl, c, xh, yk(l)))
    greeted = 4 + 3 * 5
    self_out = xl == y % 2
    for ms in range(8):
        @pl.when(jnp.logical_not(jnp.logical_and(self_out, m == ms)))
        def _():
            greet(place(z, y % 2, c, ms // 4, ms % 4))
    pl.semaphore_wait(barrier, greeted + 8 - jnp.where(self_out, 1, 0))

    send(ein_ref, ein_g.at[q0], ein_ss.at[0], ein_rs.at[q0], place(z, xl, oc, xh, y))
    send(ein_ref, ein_g.at[q0], ein_ss.at[1], ein_rs.at[q0], place(z, ox, c, xh, y))
    def attn_part(zs, j):
        return attn_g.at[zs, pl.ds(j * rows, rows)]

    def send_attn(src, zs, j, k, slot):
        send(src, attn_part(zs, j), at_ss.at[j, slot], at_rs.at[j, zs], place(zk(k), xl, c, xh, y))

    for j, k in ((0, 1), (1, 3), (1, 1), (0, 3)):
        send_attn(attn_ref.at[pl.ds(j * rows, rows)], z, j, k, k // 2)
    mine = s_g.at[q0, xh]
    send(store_ref, mine, s_ss.at[0], s_rs.at[q0, xh], place(z, ox, c, xh, y))
    send(store_ref, mine, s_ss.at[1], s_rs.at[q0, xh], place(z, xl, c, oh, y))
    send(store_ref, mine, s_ss.at[2], s_rs.at[q0, xh], place(z, ox, c, oh, y))
    send(store_ref, mine, s_ss.at[3], s_rs.at[q0, xh], place(z, xl, oc, xh, y))

    def half_cols(h):
        return pl.ds(pl.multiple_of(h * 512, 512), 512)

    def multiply_in(j, zs, q):
        res = jnp.dot(attn_g[zs, pl.ds(j * rows, rows), :], ein_g[q], preferred_element_type=F32)
        res = res.astype(BF16).reshape(4, ry, 256)
        p1[j, :, zs, :, pl.ds(pl.multiple_of(q * 256, 256), 256)] = res

    def send_partials(j, zs, hr):
        cols = half_cols(xl if hr == 0 else ox)
        for k in (1, 3, 2):
            remote(p1.at[j, yk(k), zs, :, cols], r1.at[j, hr, 3 - k, zs], r1_ss.at[j, hr, k],
                   r1_rs.at[j, hr, 3 - k], place(z, xl, c, xh, yk(k))).start()

    def unit(j, zs, hr):
        h = xl if hr == 0 else ox
        multiply_in(j, zs, h * 2 + c)
        multiply_in(j, zs, h * 2 + oc)
        send_partials(j, zs, hr)

    def attn_arrived(j, k):
        arrived(attn_part(zk(k), j), at_ss.at[j, 0], at_rs.at[j, zk(k)])

    local[0].wait()
    local[1].wait()
    for j in range(NCH):
        multiply_in(j, z, q0)
    arrived(ein_g.at[xl * 2 + oc], ein_ss.at[0], ein_rs.at[xl * 2 + oc])
    for j in range(NCH):
        multiply_in(j, z, xl * 2 + oc)
        send_partials(j, z, 0)

    pltpu.make_async_copy(eo_raw, eo_raw, loc_sem.at[3]).wait()

    @pl.loop(0, 32)
    def _(t):
        zs, ys, b = t // 8, (t // 2) % 4, t % 2
        s = ((zs // 2) * 4 + ys) * 4 + (zs % 2) * 2 + b
        eo[c, :, pl.ds(pl.multiple_of(t * BLOCK, BLOCK), BLOCK)] = eo_raw[map_ref[s]]

    send(eo.at[c], eo.at[c], eo_ss, eo_rs, place(z, xl, oc, xh, y))

    attn_arrived(0, 3)
    send_attn(attn_part(zk(3), 0), zk(3), 0, 1, 2)
    attn_arrived(1, 1)
    send_attn(attn_part(zk(1), 1), zk(1), 1, 3, 2)
    unit(0, zk(3), 0)
    unit(1, zk(1), 0)
    qa = ox * 2 + c
    arrived(ein_g.at[qa], ein_ss.at[1], ein_rs.at[qa])
    send(ein_g.at[qa], ein_g.at[qa], ein_ss.at[2], ein_rs.at[qa], place(z, xl, oc, xh, y))
    attn_arrived(1, 3)
    unit(1, zk(3), 0)
    attn_arrived(0, 1)
    unit(0, zk(1), 0)
    arrived(ein_g.at[ox * 2 + oc], ein_ss.at[2], ein_rs.at[ox * 2 + oc])
    for j in range(NCH):
        for k in (0, 1, 3):
            unit(j, zk(k), 1)
    for j in range(NCH):
        attn_arrived(j, 2)
        unit(j, zk(2), 0)
        unit(j, zk(2), 1)

    local[2].wait()
    for i, (xls, xhs) in enumerate(((ox, xh), (xl, oh), (ox, oh))):
        qs = xls * 2 + c
        arrived(s_g.at[qs, xhs], s_ss.at[0], s_rs.at[qs, xhs])
        send(s_g.at[qs, xhs], s_g.at[qs, xhs], s_ss.at[4 + i], s_rs.at[qs, xhs], place(z, xl, oc, xh, y))

    def reduce_y(j, hr):
        h = xl if hr == 0 else ox
        cols = half_cols(h)
        for k in range(3):
            arrived(r1.at[j, hr, k], r1_ss.at[j, hr, 1], r1_rs.at[j, hr, k])

        @pl.loop(0, 4)
        def _(zs):
            total = p1[j, y, zs, :, cols].astype(F32)
            for k in range(3):
                total = total + r1[j, hr, k, zs].astype(F32)
            low, high = total[:rx], total[rx:]
            ysum[j, hr, zs] = jnp.where(xh == 0, low, high)
            xs[j, hr, zs] = jnp.where(xh == 0, high, low).astype(BF16)

        send(xs.at[j, hr], xr.at[j, hr], x_ss.at[j, hr], x_rs.at[j, hr], place(z, xl, c, oh, y))

    def reduce_x(j, hr):
        h = xl if hr == 0 else ox
        arrived(xr.at[j, hr], x_ss.at[j, hr], x_rs.at[j, hr])
        total = ysum[j, hr] + xr[j, hr].astype(F32)
        a1g[j, h, y] = total.astype(BF16).reshape(4 * rx, 512)
        for k in (1, 3, 2):
            send(a1g.at[j, h, y], a1g.at[j, h, y], a1_ss.at[j, hr, k], a1_rs.at[j, hr, y],
                 place(z, xl, c, xh, yk(k)))

    def multiply_store(j):
        for hr in range(2):
            h = xl if hr == 0 else ox
            for k in range(1, 4):
                arrived(a1g.at[j, h, yk(k)], a1_ss.at[j, hr, k], a1_rs.at[j, hr, yk(k)])

        @pl.loop(0, 4)
        def _(zt):
            total = jnp.zeros((16 * rx, 256), F32)
            for q in range(4):
                lhs = a1g[j, q // 2, :, :, (q % 2) * 256:(q % 2 + 1) * 256].reshape(16 * rx, 256)
                rhs = s_g[q, zt // 2, pl.ds(pl.multiple_of((zt % 2) * 256, 256), 256), :]
                total = total + dot_nt(lhs, rhs)
            p2[j, zt] = total.astype(BF16).reshape(4, 4 * rx, 256)

        for k in range(4):
            for l in range(4):
                if k or l:
                    send(p2.at[j, zk(k), yk(l)], r2.at[j, z, y], r2_ss.at[j, k, l], r2_rs.at[j, z, y],
                         place(zk(k), xl, c, xh, yk(l)))
        r2[j, z, y] = p2[j, z, y]

    def reduce_z(j):
        for k in range(4):
            for l in range(4):
                if k or l:
                    arrived(r2.at[j, zk(k), yk(l)], r2_ss.at[j, k, l], r2_rs.at[j, zk(k), yk(l)])
        for ys in range(4):
            total = r2[j, 0, ys].astype(F32)
            for zs in range(1, 4):
                total = total + r2[j, zs, ys].astype(F32)
            a2g[j, xl, z, :, ys * 256:(ys + 1) * 256] = total.astype(BF16)
        mine = a2g.at[j, xl, z]
        send(mine, mine, a2_ss.at[j, 0], a2_rs.at[j, xl, z], place(z, ox, c, xh, y))
        for k in (1, 3, 2):
            send(mine, mine, a2_ss.at[j, k], a2_rs.at[j, xl, z], place(zk(k), xl, c, xh, y))

    def relay(j):
        near, far = pl.ds(0, 2 * rx), pl.ds(2 * rx, 2 * rx)
        arrived(a2g.at[j, ox, z], a2_ss.at[j, 0], a2_rs.at[j, ox, z])
        for k in (1, 3, 2):
            half = a2g.at[j, ox, z, near]
            send(half, half, diag_ss.at[j, 0, k], diag_rs.at[j, 0, z], place(zk(k), xl, c, xh, y))
        for k in (1, 3, 2):
            arrived(a2g.at[j, xl, zk(k)], a2_ss.at[j, k], a2_rs.at[j, xl, zk(k)])
            half = a2g.at[j, xl, zk(k), far]
            send(half, half, diag_ss.at[j, 1, k], diag_rs.at[j, 1, zk(k)], place(z, ox, c, xh, y))

    def multiply_out(j):
        near, far = pl.ds(0, 2 * rx), pl.ds(2 * rx, 2 * rx)
        for k in range(1, 4):
            arrived(a2g.at[j, ox, zk(k), near], diag_ss.at[j, 0, k], diag_rs.at[j, 0, zk(k)])
            arrived(a2g.at[j, ox, zk(k), far], diag_ss.at[j, 1, k], diag_rs.at[j, 1, zk(k)])

        @pl.loop(0, 4)
        def _(t):
            total = jnp.zeros((8 * rx, 256), F32)
            part = pl.ds(pl.multiple_of((t % 2) * 256, 256), 256)
            for zs in range(4):
                lhs = a2g[j, :, zs].reshape(8 * rx, 1024)
                total = total + dot_nt(lhs, eo[t // 2, part, zs * 1024:(zs + 1) * 1024])
            res = total.astype(BF16).reshape(2, 4, rx, 256)
            for xt in range(2):
                ob[j, :, xt, :, pl.ds(pl.multiple_of(t * 256, 256), 256)] = res[xt]

        for k in (2, 1, 3):
            send(ob.at[j, zk(k)], ow.at[j, z], ow_ss.at[j, k], ow_rs.at[j, z], place(zk(k), xl, c, xh, y))

    def out_copy(j, k, xt):
        zs = zk(k)
        src = ob.at[j, z, xt] if k == 0 else ow.at[j, zs, xt]
        dst = out_ref.at[pl.ds(pl.multiple_of(j * rows + y * ry + xh * rx, rx), rx)]
        here = jnp.logical_and(xl == xt, jnp.logical_and(zs // 2 == xh, (zs % 2) * 2 + xl == y))
        copy = remote(src, dst, out_ss.at[j, xt, k], out_rs.at[j, m], place(z, xt, c, zs // 2, (zs % 2) * 2 + xl))
        return here, copy, lambda: pltpu.make_async_copy(src, dst, out_rs.at[j, m]).start()

    def relay_out(j):
        for k in (0, 1, 3, 2):
            if k:
                arrived(ow.at[j, zk(k)], ow_ss.at[j, k], ow_rs.at[j, zk(k)])
            for xt in range(2):
                here, copy, own = out_copy(j, k, xt)

                @pl.when(here)
                def _():
                    own()

                @pl.when(jnp.logical_not(here))
                def _():
                    copy.start()

    def finish(j):
        for ms in range(8):
            dst = out_ref.at[pl.ds(j * rows + (ms % 4) * ry + (ms // 4) * rx, rx)]
            arrived(dst, out_ss.at[j, 0, 0], out_rs.at[j, ms])
        for k in range(4):
            for xt in range(2):
                here, copy, own = out_copy(j, k, xt)

                @pl.when(jnp.logical_not(here))
                def _():
                    copy.wait_send()
        for hr in range(2):
            cols = half_cols(xl if hr == 0 else ox)
            for k in range(1, 4):
                src = p1.at[j, yk(k), :, :, cols]
                remote(src, r1.at[j, hr, 3 - k], r1_ss.at[j, hr, k], r1_rs.at[j, hr, 3 - k],
                       place(z, xl, c, xh, yk(k))).wait_send()

    for j in range(NCH):
        for hr in range(2):
            reduce_y(j, hr)
            reduce_x(j, hr)
        if j == 0:
            for xls in range(2):
                for xhs in range(2):
                    qs = xls * 2 + oc
                    arrived(s_g.at[qs, xhs], s_ss.at[0], s_rs.at[qs, xhs])
    for j in range(NCH):
        multiply_store(j)
    for j in range(NCH):
        reduce_z(j)
    arrived(eo.at[oc], eo_ss, eo_rs)
    for j in range(NCH):
        relay(j)
    for j in range(NCH):
        multiply_out(j)
    for j in range(NCH):
        relay_out(j)
    for j in range(NCH):
        finish(j)
    for copy in sent:
        copy.wait_send()


def shards(old_store, block_map, expand_in, expand_out, attn, residual):
    tokens, width = attn.shape
    rows = tokens // NCH
    ry, rx = rows // 4, rows // 8
    dma = pltpu.SemaphoreType.DMA
    hbm = pl.BlockSpec(memory_space=pl.ANY)
    products = pl.pallas_call(
        chain_kernel,
        out_shape=jax.ShapeDtypeStruct((tokens, width), BF16),
        in_specs=[pl.BlockSpec(memory_space=pltpu.SMEM), hbm, hbm, hbm, hbm],
        out_specs=hbm,
        scratch_shapes=[
            pltpu.VMEM((4, tokens, width), BF16),
            pltpu.VMEM((4, width, 256), BF16),
            pltpu.VMEM((4, 2, 512, 256), BF16),
            pltpu.VMEM((32, 512, BLOCK), BF16),
            pltpu.VMEM((2, 512, 4096), BF16),
            pltpu.VMEM((NCH, 4, 4, ry, 1024), BF16),
            pltpu.VMEM((NCH, 2, 3, 4, ry, 512), BF16),
            pltpu.VMEM((NCH, 2, 4, rx, 512), F32),
            pltpu.VMEM((NCH, 2, 4, rx, 512), BF16),
            pltpu.VMEM((NCH, 2, 4, rx, 512), BF16),
            pltpu.VMEM((NCH, 2, 4, 4 * rx, 512), BF16),
            pltpu.VMEM((NCH, 4, 4, 4 * rx, 256), BF16),
            pltpu.VMEM((NCH, 4, 4, 4 * rx, 256), BF16),
            pltpu.VMEM((NCH, 2, 4, 4 * rx, 1024), BF16),
            pltpu.VMEM((NCH, 4, 2, rx, 1024), BF16),
            pltpu.VMEM((NCH, 4, 2, rx, 1024), BF16),
            dma((4,)), dma((3,)), dma((4,)), dma((7,)), dma((4, 2)),
            dma((NCH, 3)), dma((NCH, 4)), dma, dma,
            dma((NCH, 2, 4)), dma((NCH, 2, 3)), dma((NCH, 2)), dma((NCH, 2)),
            dma((NCH, 2, 4)), dma((NCH, 2, 4)), dma((NCH, 4, 4)), dma((NCH, 4, 4)),
            dma((NCH, 4)), dma((NCH, 2, 4)), dma((NCH, 2, 4)), dma((NCH, 2, 4)),
            dma((NCH, 4)), dma((NCH, 4)), dma((NCH, 2, 4)), dma((NCH, 8)),
        ],
        compiler_params=pltpu.CompilerParams(
            collective_id=0, has_side_effects=True, vmem_limit_bytes=56 * 2**20
        ),
        name="chain",
    )(block_map, old_store, expand_in, expand_out, attn)
    return (products.astype(F32) + residual.astype(F32)).astype(BF16)


def solution(mesh):
    placed = (P("mp", "dp"), P(), P("mp", "dp"), P("dp", None), P("dp", "mp"), P("dp", "mp"))
    return jax.shard_map(
        shards, mesh=mesh, in_specs=placed, out_specs=P("dp", "mp"), check_vma=False
    )
```

```python
import jax
import jax.numpy as jnp
from jax import lax
from jax.experimental import pallas as pl
from jax.experimental.pallas import tpu as pltpu
from jax.sharding import PartitionSpec as P

MESH = pl.DeviceIdType.MESH
BLOCK = 128
NCH = 2
NEAR = 32
F32 = jnp.float32
BF16 = jnp.bfloat16


def place(z, xl, c, xh, y):
    return {"dp": z * 4 + xl * 2 + c, "mp": xh * 4 + y}


def dot_nt(a, b):
    return lax.dot_general(a, b, (((1,), (1,)), ((), ())), preferred_element_type=F32)


def chain_kernel(
    map_ref, store_ref, ein_ref, eout_ref, attn_ref, out_ref,
    attn_g, ein_g, s_g, eo_raw, eo, p1, r1, ysum, xs, xr, a1g, p2, r2, rm, q2, a2g, ob, ow,
    loc_sem, ein_ss, ein_rs, s_ss, s_rs, at_ss, at_rs, eo_ss, eo_rs, r1_ss, r1_rs, x_ss, x_rs,
    a1_ss, a1_rs, r2_ss, r2_rs, rm_ss, rm_rs, q2_ss, q2_rs, a2_ss, a2_rs, diag_ss, diag_rs, ow_ss, ow_rs, out_ss, out_rs,
):
    d = lax.axis_index("dp")
    m = lax.axis_index("mp")
    z, xl, c = d // 4, (d // 2) % 2, d % 2
    xh, y = m // 4, m % 4
    q0 = xl * 2 + c
    ox, oc, oh = 1 - xl, 1 - c, 1 - xh
    rows = attn_ref.shape[0] // NCH
    ry, rx = rows // 4, rows // 8
    sent = []

    def remote(src, dst, ss, rs, target):
        return pltpu.make_async_remote_copy(
            src_ref=src, dst_ref=dst, send_sem=ss, recv_sem=rs, device_id=target, device_id_type=MESH
        )

    def send(src, dst, ss, rs, target):
        copy = remote(src, dst, ss, rs, target)
        copy.start()
        sent.append(copy)

    def arrived(dst, ss, rs):
        remote(dst, dst, ss, rs, place(z, xl, oc, xh, y)).wait_recv()

    def zk(k):
        return lax.rem(z + k, 4)

    def yk(k):
        return lax.rem(y + k, 4)

    local = [
        pltpu.make_async_copy(attn_ref, attn_g.at[z], loc_sem.at[0]),
        pltpu.make_async_copy(ein_ref.at[:, :128], ein_g.at[q0, 0], loc_sem.at[1]),
        pltpu.make_async_copy(ein_ref.at[:, 128:], ein_g.at[q0, 1], loc_sem.at[4]),
        pltpu.make_async_copy(store_ref, s_g.at[q0, xh], loc_sem.at[2]),
    ]
    for copy in local:
        copy.start()

    @pl.loop(0, 32)
    def _(t):
        cols = pl.ds(pl.multiple_of(t * BLOCK, BLOCK), BLOCK)
        pltpu.make_async_copy(eout_ref.at[:, cols], eo_raw.at[t], loc_sem.at[3]).start()

    barrier = pltpu.get_barrier_semaphore()

    def greet(target):
        pl.semaphore_signal(barrier, inc=1, device_id=target, device_id_type=MESH)

    greet(place(z, xl, oc, xh, y))
    greet(place(z, ox, c, xh, y))
    greet(place(z, xl, c, oh, y))
    greet(place(z, ox, c, oh, y))
    for k in range(1, 4):
        greet(place(z, xl, c, xh, yk(k)))
        greet(place(zk(k), xl, c, xh, y))
    pl.semaphore_wait(barrier, 10)

    for a in range(2):
        src = ein_ref.at[:, a * 128:(a + 1) * 128]
        send(src, ein_g.at[q0, a], ein_ss.at[a, 0], ein_rs.at[q0, a], place(z, xl, oc, xh, y))
        send(src, ein_g.at[q0, a], ein_ss.at[a, 1], ein_rs.at[q0, a], place(z, ox, c, xh, y))

    def attn_part(zs, j):
        return attn_g.at[zs, pl.ds(j * rows, rows)]

    def send_attn(j):
        for k in (1, 3):
            send(attn_ref.at[pl.ds(j * rows, rows)], attn_part(z, j), at_ss.at[j, k], at_rs.at[j, z],
                 place(zk(k), xl, c, xh, y))

    def attn_arrived(j, k):
        arrived(attn_part(zk(k), j), at_ss.at[j, k], at_rs.at[j, zk(k)])

    def attn_near(j):
        half = rows // 2
        for k in (1, 3):
            attn_arrived(j, 4 - k)
            src = attn_g.at[zk(4 - k), pl.ds(j * rows + (k // 2) * half, half)]
            send(src, src, at_ss.at[j, k - 1], at_rs.at[j, zk(4 - k)], place(zk(k), xl, c, xh, y))

    send_attn(0)

    mine = s_g.at[q0, xh]
    send(store_ref, mine, s_ss.at[0], s_rs.at[q0, xh], place(z, ox, c, oh, y))
    send(store_ref, mine, s_ss.at[1], s_rs.at[q0, xh], place(z, xl, oc, xh, y))

    def half_cols(h):
        return pl.ds(pl.multiple_of(h * 512, 512), 512)

    def multiply_in(j, zs, hr, a):
        h = xl if hr == 0 else ox
        rhs = jnp.concatenate([ein_g[h * 2, a], ein_g[h * 2 + 1, a]], axis=1)
        res = jnp.dot(attn_g[zs, pl.ds(j * rows, rows), :], rhs, preferred_element_type=F32)
        res = res.astype(BF16).reshape(4, ry, 256)
        p1[j, :, zs, :, pl.ds(pl.multiple_of(h * 512 + a * 256, 256), 256)] = res

    def send_partials(j, zs, hr, first=0, width=512):
        cols = pl.ds(pl.multiple_of((xl if hr == 0 else ox) * 512 + first, 256), width)
        for k in (1, 3, 2):
            remote(p1.at[j, yk(k), zs, :, cols], r1.at[j, hr, 3 - k, zs, :, first:first + width],
                   r1_ss.at[j, hr, k], r1_rs.at[j, hr, 3 - k], place(z, xl, c, xh, yk(k))).start()

    def unit(j, zs, hr, a=None):
        if a is None:
            multiply_in(j, zs, hr, 0)
            multiply_in(j, zs, hr, 1)
            send_partials(j, zs, hr)
        else:
            multiply_in(j, zs, hr, a)
            send_partials(j, zs, hr, a * 256, 256)

    def compute(j, zs, hr):
        multiply_in(j, zs, hr, 0)
        multiply_in(j, zs, hr, 1)

    def ein_far(a):
        qa = ox * 2 + c
        arrived(ein_g.at[qa, a], ein_ss.at[a, 1], ein_rs.at[qa, a])
        send(ein_g.at[qa, a], ein_g.at[qa, a], ein_ss.at[a, 2], ein_rs.at[qa, a], place(z, xl, oc, xh, y))

    def ein_far_core(a):
        qb = ox * 2 + oc
        arrived(ein_g.at[qb, a], ein_ss.at[a, 2], ein_rs.at[qb, a])

    def send_store():
        send(store_ref, mine, s_ss.at[2], s_rs.at[q0, xh], place(z, ox, c, xh, y))

    def relay_store(i, xls, xhs):
        block = s_g.at[xls * 2 + c, xhs]
        arrived(block, s_ss.at[0], s_rs.at[xls * 2 + c, xhs])
        send(block, block, s_ss.at[3 + i], s_rs.at[xls * 2 + c, xhs], place(z, xl, oc, xh, y))
        if i == 1:
            send(block, block, s_ss.at[6], s_rs.at[xls * 2 + c, xhs], place(z, ox, c, oh, y))

    local[0].wait()
    local[1].wait()
    local[2].wait()
    for a in range(2):
        arrived(ein_g.at[xl * 2 + oc, a], ein_ss.at[a, 0], ein_rs.at[xl * 2 + oc, a])
    unit(0, z, 0)
    unit(1, z, 0)

    pltpu.make_async_copy(eo_raw, eo_raw, loc_sem.at[3]).wait()

    @pl.loop(0, 32)
    def _(t):
        zs, ys, b = t // 8, (t // 2) % 4, t % 2
        s = ((zs // 2) * 4 + ys) * 4 + (zs % 2) * 2 + b
        eo[c, pl.ds(pl.multiple_of(t * BLOCK, BLOCK), BLOCK), :] = eo_raw[map_ref[s]].T

    send(eo.at[c], eo.at[c], eo_ss, eo_rs, place(z, xl, oc, xh, y))

    attn_near(0)
    send_attn(1)
    unit(0, zk(1), 0)
    unit(0, zk(3), 0)
    ein_far(0)
    ein_far_core(0)
    for k in (0, 1, 3):
        unit(0, zk(k), 1, 0)
    attn_arrived(0, 2)
    unit(0, zk(2), 0)
    unit(0, zk(2), 1, 0)
    ein_far(1)
    send_store()
    ein_far_core(1)
    for k in range(4):
        unit(0, zk(k), 1, 1)
    unit(1, z, 1)
    relay_store(0, ox, oh)
    attn_near(1)

    def store_arrived():
        local[3].wait()
        for xls in range(2):
            for xhs in range(2):
                qs = xls * 2 + oc
                arrived(s_g.at[qs, xhs], s_ss.at[0], s_rs.at[qs, xhs])

    def reduce_y(j, hr):
        h = xl if hr == 0 else ox
        cols = half_cols(h)
        for k in range(3):
            arrived(r1.at[j, hr, k], r1_ss.at[j, hr, 1], r1_rs.at[j, hr, k])

        @pl.loop(0, 4)
        def _(zs):
            total = p1[j, y, zs, :, cols].astype(F32)
            for k in range(3):
                total = total + r1[j, hr, k, zs].astype(F32)
            low, high = total[:rx], total[rx:]
            ysum[j, hr, zs] = jnp.where(xh == 0, low, high)
            xs[j, hr, zs] = jnp.where(xh == 0, high, low).astype(BF16)

        send(xs.at[j, hr], xr.at[j, hr], x_ss.at[j, hr], x_rs.at[j, hr], place(z, xl, c, oh, y))

    def reduce_x(j, hr):
        h = xl if hr == 0 else ox
        arrived(xr.at[j, hr], x_ss.at[j, hr], x_rs.at[j, hr])
        total = ysum[j, hr] + xr[j, hr].astype(F32)
        a1g[j, h, y] = total.astype(BF16).reshape(4 * rx, 512)
        for k in (1, 3, 2):
            send(a1g.at[j, h, y], a1g.at[j, h, y], a1_ss.at[j, hr, k], a1_rs.at[j, hr, y],
                 place(z, xl, c, xh, yk(k)))

    def multiply_store(j):
        for hr in range(2):
            h = xl if hr == 0 else ox
            for k in range(1, 4):
                arrived(a1g.at[j, h, yk(k)], a1_ss.at[j, hr, k], a1_rs.at[j, hr, yk(k)])

        for k in (2, 1, 3, 0):
            zt = zk(k)
            total = jnp.zeros((16 * rx, 256), F32)
            for q in range(4):
                first = (q % 2) * 128
                lhs = jnp.concatenate(
                    [a1g[j, q // 2, :, :, first:first + 128], a1g[j, q // 2, :, :, first + 256:first + 384]], axis=2
                ).reshape(16 * rx, 256)
                rhs = s_g[q, zt // 2, pl.ds(pl.multiple_of((zt % 2) * 256, 256), 256), :]
                total = total + dot_nt(lhs, rhs)
            p2[j, zt] = total.astype(BF16).reshape(4, 4 * rx, 256)
            if j == 0:
                if k:
                    send(p2.at[j, zt], r2.at[3 - k], r2_ss.at[k], r2_rs.at[3 - k], place(zt, xl, c, xh, y))
            else:
                for l in (2, 1, 3, 0):
                    if k or l:
                        send(p2.at[j, zt, yk(l)], rm.at[z, y], rm_ss.at[k, l], rm_rs.at[z, y],
                             place(zt, xl, c, xh, yk(l)))

    def a2_cols(ys):
        return pl.ds(pl.multiple_of(ys * 256, 256), 256)

    def reduce_z():
        for k in range(1, 4):
            arrived(r2.at[3 - k], r2_ss.at[k], r2_rs.at[3 - k])

        @pl.loop(0, 4)
        def _(yt):
            total = p2[0, z, yt].astype(F32)
            for k in range(3):
                total = total + r2[k, yt].astype(F32)
            q2[yt] = total.astype(BF16)

        for k in (2, 1, 3):
            send(q2.at[yk(k)], a2g.at[0, xl, z, :, a2_cols(y)], q2_ss.at[k], q2_rs.at[y], place(z, xl, c, xh, yk(k)))
        a2g[0, xl, z, :, a2_cols(y)] = q2[y]

    def reduce_zy():
        rm[z, y] = p2[1, z, y]
        for k in range(4):
            for l in range(4):
                if k or l:
                    arrived(rm.at[zk(k), yk(l)], rm_ss.at[k, l], rm_rs.at[zk(k), yk(l)])

        @pl.loop(0, 4)
        def _(ys):
            total = rm[0, ys].astype(F32)
            for zs in range(1, 4):
                total = total + rm[zs, ys].astype(F32)
            a2g[1, xl, z, :, a2_cols(ys)] = total.astype(BF16)

    def spread(j):
        if j == 0:
            for k in range(1, 4):
                arrived(a2g.at[j, xl, z, :, a2_cols(yk(k))], q2_ss.at[k], q2_rs.at[yk(k)])
        for half in (0, 1):
            to_x, to_z = a2g.at[j, xl, z, parts[half]], a2g.at[j, xl, z, parts[1 - half]]
            send(to_x, to_x, a2_ss.at[j, half, 0], a2_rs.at[j, half, xl, z], place(z, ox, c, xh, y))
            for k in (1, 3, 2):
                send(to_z, to_z, a2_ss.at[j, 1 - half, k], a2_rs.at[j, 1 - half, xl, z], place(zk(k), xl, c, xh, y))

    parts = (pl.ds(0, NEAR), pl.ds(NEAR, 4 * rx - NEAR))

    def block_arrived(j, half, xs_, k):
        arrived(a2g.at[j, xs_, zk(k), parts[half]], a2_ss.at[j, half, k], a2_rs.at[j, half, xs_, zk(k)])

    def relay_x(j):
        block_arrived(j, 0, ox, 0)
        for k in (1, 3, 2):
            half = a2g.at[j, ox, z, parts[0]]
            send(half, half, diag_ss.at[j, 0, k], diag_rs.at[j, 0, z], place(zk(k), xl, c, xh, y))

    def relay_z(j):
        for k in (1, 3, 2):
            block_arrived(j, 1, xl, k)
            half = a2g.at[j, xl, zk(k), parts[1]]
            send(half, half, diag_ss.at[j, 1, k], diag_rs.at[j, 1, zk(k)], place(z, ox, c, xh, y))

    def multiply_out(j):
        block_arrived(j, 1, ox, 0)
        for k in range(1, 4):
            block_arrived(j, 0, xl, k)
            for half in range(2):
                arrived(a2g.at[j, ox, zk(k), parts[half]], diag_ss.at[j, half, k], diag_rs.at[j, half, zk(k)])
        for half in range(2):
            @pl.loop(0, 2)
            def _(t):
                total = jnp.zeros((8 * rx, 256), F32)
                part = pl.ds(pl.multiple_of(t * 256, 256), 256)
                for zs in range(4):
                    lhs = a2g[j, :, zs].reshape(8 * rx, 1024)
                    rhs = eo[half, zs * 1024:(zs + 1) * 1024, part]
                    total = total + jnp.dot(lhs, rhs, preferred_element_type=F32)
                res = total.astype(BF16).reshape(2, 4, rx, 256)
                for xt in range(2):
                    ob[j, half, :, xt, :, part] = res[xt]

            for k in (2, 1, 3):
                send(ob.at[j, half, zk(k)], ow.at[j, half, z], ow_ss.at[j, half, k], ow_rs.at[j, half, z],
                     place(zk(k), xl, c, xh, y))

    def out_copy(j, half, k, xt):
        zs = zk(k)
        src = ow.at[j, half, zs, xt] if k else ob.at[j, half, z, xt]
        dst = out_ref.at[pl.ds(pl.multiple_of(j * rows + y * ry + xh * rx, rx), rx), pl.ds(half * 512, 512)]
        here = jnp.logical_and(xl == xt, jnp.logical_and(zs // 2 == xh, (zs % 2) * 2 + xl == y))
        copy = remote(src, dst, out_ss.at[j, half, k, xt], out_rs.at[j, half, m],
                      place(z, xt, c, zs // 2, (zs % 2) * 2 + xl))
        return here, copy, lambda: pltpu.make_async_copy(src, dst, out_rs.at[j, half, m]).start()

    def relay_out(j, half):
        for k in (0, 1, 3, 2):
            if k:
                arrived(ow.at[j, half, zk(k)], ow_ss.at[j, half, k], ow_rs.at[j, half, zk(k)])
            for xt in range(2):
                here, copy, own = out_copy(j, half, k, xt)
                pl.when(here)(own)
                pl.when(jnp.logical_not(here))(copy.start)

    def finish(j):
        for half in range(2):
            for ms in range(8):
                dst = out_ref.at[pl.ds(j * rows + (ms % 4) * ry + (ms // 4) * rx, rx), pl.ds(half * 512, 512)]
                arrived(dst, out_ss.at[j, 0, 0, 0], out_rs.at[j, half, ms])
            for k in range(4):
                for xt in range(2):
                    here, copy, own = out_copy(j, half, k, xt)
                    pl.when(jnp.logical_not(here))(copy.wait_send)
        for hr in range(2):
            cols = half_cols(xl if hr == 0 else ox)
            for k in range(1, 4):
                remote(p1.at[j, yk(k), :, :, cols], r1.at[j, hr, 3 - k], r1_ss.at[j, hr, k], r1_rs.at[j, hr, 3 - k],
                       place(z, xl, c, xh, yk(k))).wait_send()

    reduce_y(0, 0)
    relay_store(1, ox, xh)
    compute(1, zk(1), 0)
    compute(1, zk(3), 0)
    reduce_x(0, 0)
    send_partials(1, zk(1), 0)
    compute(1, zk(1), 1)
    compute(1, zk(3), 1)
    reduce_y(0, 1)
    attn_arrived(1, 2)
    compute(1, zk(2), 0)
    compute(1, zk(2), 1)
    reduce_x(0, 1)
    for hr in range(2):
        for k in (1, 3, 2):
            if k != 1 or hr != 0:
                send_partials(1, zk(k), hr)
    relay_store(2, xl, oh)
    store_arrived()
    multiply_store(0)
    reduce_y(1, 0)
    reduce_y(1, 1)
    reduce_x(1, 0)
    reduce_z()
    reduce_x(1, 1)
    spread(0)
    relay_x(0)
    multiply_store(1)
    relay_z(0)
    reduce_zy()
    spread(1)
    arrived(eo.at[oc], eo_ss, eo_rs)
    relay_x(1)
    multiply_out(0)
    relay_z(1)
    relay_out(0, 0)
    relay_out(0, 1)
    multiply_out(1)
    relay_out(1, 0)
    relay_out(1, 1)
    for j in range(NCH):
        finish(j)
    for copy in sent:
        copy.wait_send()


def shards(old_store, block_map, expand_in, expand_out, attn, residual):
    tokens, width = attn.shape
    rows = tokens // NCH
    ry, rx = rows // 4, rows // 8
    dma = pltpu.SemaphoreType.DMA
    hbm = pl.BlockSpec(memory_space=pl.ANY)
    products = pl.pallas_call(
        chain_kernel,
        out_shape=jax.ShapeDtypeStruct((tokens, width), BF16),
        in_specs=[pl.BlockSpec(memory_space=pltpu.SMEM), hbm, hbm, hbm, hbm],
        out_specs=hbm,
        scratch_shapes=[
            pltpu.VMEM((4, tokens, width), BF16),
            pltpu.VMEM((4, 2, width, 128), BF16),
            pltpu.VMEM((4, 2, 512, 256), BF16),
            pltpu.VMEM((32, 512, BLOCK), BF16),
            pltpu.VMEM((2, 4096, 512), BF16),
            pltpu.VMEM((NCH, 4, 4, ry, 1024), BF16),
            pltpu.VMEM((NCH, 2, 3, 4, ry, 512), BF16),
            pltpu.VMEM((NCH, 2, 4, rx, 512), F32),
            pltpu.VMEM((NCH, 2, 4, rx, 512), BF16),
            pltpu.VMEM((NCH, 2, 4, rx, 512), BF16),
            pltpu.VMEM((NCH, 2, 4, 4 * rx, 512), BF16),
            pltpu.VMEM((NCH, 4, 4, 4 * rx, 256), BF16),
            pltpu.VMEM((3, 4, 4 * rx, 256), BF16),
            pltpu.VMEM((4, 4, 4 * rx, 256), BF16),
            pltpu.VMEM((4, 4 * rx, 256), BF16),
            pltpu.VMEM((NCH, 2, 4, 4 * rx, 1024), BF16),
            pltpu.VMEM((NCH, 2, 4, 2, rx, 512), BF16),
            pltpu.VMEM((NCH, 2, 4, 2, rx, 512), BF16),
            dma((5,)), dma((2, 3)), dma((4, 2)), dma((7,)), dma((4, 2)),
            dma((NCH, 4)), dma((NCH, 4)), dma, dma,
            dma((NCH, 2, 4)), dma((NCH, 2, 3)), dma((NCH, 2)), dma((NCH, 2)),
            dma((NCH, 2, 4)), dma((NCH, 2, 4)), dma((4,)), dma((3,)), dma((4, 4)), dma((4, 4)), dma((4,)), dma((4,)),
            dma((NCH, 2, 4)), dma((NCH, 2, 2, 4)), dma((NCH, 2, 4)), dma((NCH, 2, 4)),
            dma((NCH, 2, 4)), dma((NCH, 2, 4)), dma((NCH, 2, 4, 2)), dma((NCH, 2, 8)),
        ],
        compiler_params=pltpu.CompilerParams(
            collective_id=0, has_side_effects=True, vmem_limit_bytes=56 * 2**20
        ),
        name="chain",
    )(block_map, old_store, expand_in, expand_out, attn)
    return (products.astype(F32) + residual.astype(F32)).astype(BF16)


def solution(mesh):
    placed = (P("mp", "dp"), P(), P("mp", "dp"), P("dp", None), P("dp", "mp"), P("dp", "mp"))
    return jax.shard_map(
        shards, mesh=mesh, in_specs=placed, out_specs=P("dp", "mp"), check_vma=False
    )
```

```python
import jax
import jax.numpy as jnp
from jax import lax
from jax.experimental import pallas as pl
from jax.experimental.pallas import tpu as pltpu
from jax.sharding import PartitionSpec as P

MESH = pl.DeviceIdType.MESH
BLOCK = 128
NCH = 2
NEAR = 32
F32 = jnp.float32
BF16 = jnp.bfloat16


def place(z, xl, c, xh, y):
    return {"dp": z * 4 + xl * 2 + c, "mp": xh * 4 + y}


def dot_nt(a, b):
    return lax.dot_general(a, b, (((1,), (1,)), ((), ())), preferred_element_type=F32)


def chain_kernel(
    map_ref, store_ref, ein_ref, eout_ref, attn_ref, out_ref,
    attn_g, ein_g, s_g, eo_raw, eo, p1, r1, ysum, xs, xr, a1g, p2, r2, rm, q2, a2g, ob, ow,
    loc_sem, ein_ss, ein_rs, s_ss, s_rs, at_ss, at_rs, eo_ss, eo_rs, r1_ss, r1_rs, x_ss, x_rs,
    a1_ss, a1_rs, r2_ss, r2_rs, rm_ss, rm_rs, q2_ss, q2_rs, a2_ss, a2_rs, diag_ss, diag_rs, ow_ss, ow_rs, out_ss, out_rs,
):
    d = lax.axis_index("dp")
    m = lax.axis_index("mp")
    z, xl, c = d // 4, (d // 2) % 2, d % 2
    xh, y = m // 4, m % 4
    q0 = xl * 2 + c
    ox, oc, oh = 1 - xl, 1 - c, 1 - xh
    rows = attn_ref.shape[0] // NCH
    ry, rx = rows // 4, rows // 8
    sent = []

    def remote(src, dst, ss, rs, target):
        return pltpu.make_async_remote_copy(
            src_ref=src, dst_ref=dst, send_sem=ss, recv_sem=rs, device_id=target, device_id_type=MESH
        )

    def send(src, dst, ss, rs, target):
        copy = remote(src, dst, ss, rs, target)
        copy.start()
        sent.append(copy)

    def arrived(dst, ss, rs):
        remote(dst, dst, ss, rs, place(z, xl, oc, xh, y)).wait_recv()

    def zk(k):
        return lax.rem(z + k, 4)

    def yk(k):
        return lax.rem(y + k, 4)

    local = [
        pltpu.make_async_copy(attn_ref, attn_g.at[z], loc_sem.at[0]),
        pltpu.make_async_copy(ein_ref.at[:, :128], ein_g.at[q0, 0], loc_sem.at[1]),
        pltpu.make_async_copy(ein_ref.at[:, 128:], ein_g.at[q0, 1], loc_sem.at[4]),
        pltpu.make_async_copy(store_ref, s_g.at[q0, xh], loc_sem.at[2]),
    ]
    for copy in local:
        copy.start()

    @pl.loop(0, 32)
    def _(t):
        cols = pl.ds(pl.multiple_of(t * BLOCK, BLOCK), BLOCK)
        pltpu.make_async_copy(eout_ref.at[:, cols], eo_raw.at[t], loc_sem.at[3]).start()

    barrier = pltpu.get_barrier_semaphore()

    def greet(target):
        pl.semaphore_signal(barrier, inc=1, device_id=target, device_id_type=MESH)

    greet(place(z, xl, oc, xh, y))
    greet(place(z, ox, c, xh, y))
    greet(place(z, xl, c, oh, y))
    greet(place(z, ox, c, oh, y))
    for k in range(1, 4):
        greet(place(z, xl, c, xh, yk(k)))
        greet(place(zk(k), xl, c, xh, y))
    pl.semaphore_wait(barrier, 10)

    for a in range(2):
        src = ein_ref.at[:, a * 128:(a + 1) * 128]
        send(src, ein_g.at[q0, a], ein_ss.at[a, 0], ein_rs.at[q0, a], place(z, xl, oc, xh, y))
        send(src, ein_g.at[q0, a], ein_ss.at[a, 1], ein_rs.at[q0, a], place(z, ox, c, xh, y))

    def attn_part(zs, j):
        return attn_g.at[zs, pl.ds(j * rows, rows)]

    def send_attn(j):
        for k in (1, 3):
            send(attn_ref.at[pl.ds(j * rows, rows)], attn_part(z, j), at_ss.at[j, k], at_rs.at[j, z],
                 place(zk(k), xl, c, xh, y))

    def attn_arrived(j, k):
        arrived(attn_part(zk(k), j), at_ss.at[j, k], at_rs.at[j, zk(k)])

    def attn_near(j):
        half = rows // 2
        for k in (1, 3):
            attn_arrived(j, 4 - k)
            src = attn_g.at[zk(4 - k), pl.ds(j * rows + (k // 2) * half, half)]
            send(src, src, at_ss.at[j, k - 1], at_rs.at[j, zk(4 - k)], place(zk(k), xl, c, xh, y))

    send_attn(0)

    mine = s_g.at[q0, xh]
    send(store_ref, mine, s_ss.at[0], s_rs.at[q0, xh], place(z, ox, c, oh, y))
    send(store_ref, mine, s_ss.at[1], s_rs.at[q0, xh], place(z, xl, oc, xh, y))

    def half_cols(h):
        return pl.ds(pl.multiple_of(h * 512, 512), 512)

    def multiply_in(j, zs, hr, a):
        h = xl if hr == 0 else ox
        rhs = jnp.concatenate([ein_g[h * 2, a], ein_g[h * 2 + 1, a]], axis=1)
        res = jnp.dot(attn_g[zs, pl.ds(j * rows, rows), :], rhs, preferred_element_type=F32)
        res = res.astype(BF16).reshape(4, ry, 256)
        p1[j, :, zs, :, pl.ds(pl.multiple_of(h * 512 + a * 256, 256), 256)] = res

    def send_partials(j, zs, hr, first=0, width=512):
        cols = pl.ds(pl.multiple_of((xl if hr == 0 else ox) * 512 + first, 256), width)
        for k in (1, 3, 2):
            remote(p1.at[j, yk(k), zs, :, cols], r1.at[j, hr, 3 - k, zs, :, first:first + width],
                   r1_ss.at[j, hr, k], r1_rs.at[j, hr, 3 - k], place(z, xl, c, xh, yk(k))).start()

    def unit(j, zs, hr, a=None):
        if a is None:
            multiply_in(j, zs, hr, 0)
            multiply_in(j, zs, hr, 1)
            send_partials(j, zs, hr)
        else:
            multiply_in(j, zs, hr, a)
            send_partials(j, zs, hr, a * 256, 256)

    def compute(j, zs, hr):
        multiply_in(j, zs, hr, 0)
        multiply_in(j, zs, hr, 1)

    def ein_far(a):
        qa = ox * 2 + c
        arrived(ein_g.at[qa, a], ein_ss.at[a, 1], ein_rs.at[qa, a])
        send(ein_g.at[qa, a], ein_g.at[qa, a], ein_ss.at[a, 2], ein_rs.at[qa, a], place(z, xl, oc, xh, y))

    def ein_far_core(a):
        qb = ox * 2 + oc
        arrived(ein_g.at[qb, a], ein_ss.at[a, 2], ein_rs.at[qb, a])

    def send_store():
        send(store_ref, mine, s_ss.at[2], s_rs.at[q0, xh], place(z, ox, c, xh, y))

    def relay_store(i, xls, xhs):
        block = s_g.at[xls * 2 + c, xhs]
        arrived(block, s_ss.at[0], s_rs.at[xls * 2 + c, xhs])
        send(block, block, s_ss.at[3 + i], s_rs.at[xls * 2 + c, xhs], place(z, xl, oc, xh, y))
        if i == 1:
            send(block, block, s_ss.at[6], s_rs.at[xls * 2 + c, xhs], place(z, ox, c, oh, y))

    local[0].wait()
    local[1].wait()
    local[2].wait()
    for a in range(2):
        arrived(ein_g.at[xl * 2 + oc, a], ein_ss.at[a, 0], ein_rs.at[xl * 2 + oc, a])
    unit(0, z, 0)
    unit(1, z, 0)

    pltpu.make_async_copy(eo_raw, eo_raw, loc_sem.at[3]).wait()

    @pl.loop(0, 32)
    def _(t):
        zs, ys, b = t // 8, (t // 2) % 4, t % 2
        s = ((zs // 2) * 4 + ys) * 4 + (zs % 2) * 2 + b
        eo[c, pl.ds(pl.multiple_of(t * BLOCK, BLOCK), BLOCK), :] = eo_raw[map_ref[s]].T

    attn_near(0)
    send_attn(1)
    unit(0, zk(1), 0)
    unit(0, zk(3), 0)
    ein_far(0)
    ein_far_core(0)
    for k in (0, 1, 3):
        unit(0, zk(k), 1, 0)
    attn_arrived(0, 2)
    unit(0, zk(2), 0)
    unit(0, zk(2), 1, 0)
    ein_far(1)
    send_store()
    ein_far_core(1)
    for k in range(4):
        unit(0, zk(k), 1, 1)
    unit(1, z, 1)
    relay_store(0, ox, oh)
    attn_near(1)

    def store_arrived():
        local[3].wait()
        for xls in range(2):
            for xhs in range(2):
                qs = xls * 2 + oc
                arrived(s_g.at[qs, xhs], s_ss.at[0], s_rs.at[qs, xhs])

    def reduce_y(j, hr):
        h = xl if hr == 0 else ox
        cols = half_cols(h)
        for k in range(3):
            arrived(r1.at[j, hr, k], r1_ss.at[j, hr, 1], r1_rs.at[j, hr, k])

        @pl.loop(0, 4)
        def _(zs):
            total = p1[j, y, zs, :, cols].astype(F32)
            for k in range(3):
                total = total + r1[j, hr, k, zs].astype(F32)
            low, high = total[:rx], total[rx:]
            ysum[j, hr, zs] = jnp.where(xh == 0, low, high)
            xs[j, hr, zs] = jnp.where(xh == 0, high, low).astype(BF16)

        send(xs.at[j, hr], xr.at[j, hr], x_ss.at[j, hr], x_rs.at[j, hr], place(z, xl, c, oh, y))

    def reduce_x(j, hr):
        h = xl if hr == 0 else ox
        arrived(xr.at[j, hr], x_ss.at[j, hr], x_rs.at[j, hr])
        total = ysum[j, hr] + xr[j, hr].astype(F32)
        a1g[j, h, y] = total.astype(BF16).reshape(4 * rx, 512)
        for k in (2, 1, 3):
            send(a1g.at[j, h, y], a1g.at[j, h, y], a1_ss.at[j, hr, k], a1_rs.at[j, hr, y],
                 place(z, xl, c, xh, yk(k)))

    def multiply_store(j):
        for hr in range(2):
            h = xl if hr == 0 else ox
            for k in range(1, 4):
                arrived(a1g.at[j, h, yk(k)], a1_ss.at[j, hr, k], a1_rs.at[j, hr, yk(k)])

        for k in (2, 1, 3, 0):
            zt = zk(k)
            total = jnp.zeros((16 * rx, 256), F32)
            for q in range(4):
                first = (q % 2) * 128
                lhs = jnp.concatenate(
                    [a1g[j, q // 2, :, :, first:first + 128], a1g[j, q // 2, :, :, first + 256:first + 384]], axis=2
                ).reshape(16 * rx, 256)
                rhs = s_g[q, zt // 2, pl.ds(pl.multiple_of((zt % 2) * 256, 256), 256), :]
                total = total + dot_nt(lhs, rhs)
            p2[j, zt] = total.astype(BF16).reshape(4, 4 * rx, 256)
            if j == 0:
                if k:
                    send(p2.at[j, zt], r2.at[3 - k], r2_ss.at[k], r2_rs.at[3 - k], place(zt, xl, c, xh, y))
            else:
                for l in (2, 1, 3, 0):
                    if k or l:
                        send(p2.at[j, zt, yk(l)], rm.at[z, y], rm_ss.at[k, l], rm_rs.at[z, y],
                             place(zt, xl, c, xh, yk(l)))

    def a2_cols(ys):
        return pl.ds(pl.multiple_of(ys * 256, 256), 256)

    def reduce_z():
        for k in range(1, 4):
            arrived(r2.at[3 - k], r2_ss.at[k], r2_rs.at[3 - k])

        @pl.loop(0, 4)
        def _(yt):
            total = p2[0, z, yt].astype(F32)
            for k in range(3):
                total = total + r2[k, yt].astype(F32)
            q2[yt] = total.astype(BF16)

        for k in (2, 1, 3):
            send(q2.at[yk(k)], a2g.at[0, xl, z, :, a2_cols(y)], q2_ss.at[k], q2_rs.at[y], place(z, xl, c, xh, yk(k)))
        a2g[0, xl, z, :, a2_cols(y)] = q2[y]

    def reduce_zy():
        rm[z, y] = p2[1, z, y]
        for k in range(4):
            for l in range(4):
                if k or l:
                    arrived(rm.at[zk(k), yk(l)], rm_ss.at[k, l], rm_rs.at[zk(k), yk(l)])

        @pl.loop(0, 4)
        def _(ys):
            total = rm[0, ys].astype(F32)
            for zs in range(1, 4):
                total = total + rm[zs, ys].astype(F32)
            a2g[1, xl, z, :, a2_cols(ys)] = total.astype(BF16)

    def spread(j):
        if j == 0:
            for k in range(1, 4):
                arrived(a2g.at[j, xl, z, :, a2_cols(yk(k))], q2_ss.at[k], q2_rs.at[yk(k)])
        for half in (0, 1):
            to_x, to_z = a2g.at[j, xl, z, parts[half]], a2g.at[j, xl, z, parts[1 - half]]
            send(to_x, to_x, a2_ss.at[j, half, 0], a2_rs.at[j, half, xl, z], place(z, ox, c, xh, y))
            for k in (1, 3, 2):
                send(to_z, to_z, a2_ss.at[j, 1 - half, k], a2_rs.at[j, 1 - half, xl, z], place(zk(k), xl, c, xh, y))

    parts = (pl.ds(0, NEAR), pl.ds(NEAR, 4 * rx - NEAR))

    def block_arrived(j, half, xs_, k):
        arrived(a2g.at[j, xs_, zk(k), parts[half]], a2_ss.at[j, half, k], a2_rs.at[j, half, xs_, zk(k)])

    def relay_x(j):
        block_arrived(j, 0, ox, 0)
        for k in (1, 3, 2):
            half = a2g.at[j, ox, z, parts[0]]
            send(half, half, diag_ss.at[j, 0, k], diag_rs.at[j, 0, z], place(zk(k), xl, c, xh, y))

    def relay_z(j):
        for k in (1, 3, 2):
            block_arrived(j, 1, xl, k)
            half = a2g.at[j, xl, zk(k), parts[1]]
            send(half, half, diag_ss.at[j, 1, k], diag_rs.at[j, 1, zk(k)], place(z, ox, c, xh, y))

    def multiply_out(j):
        block_arrived(j, 1, ox, 0)
        for k in range(1, 4):
            block_arrived(j, 0, xl, k)
            for half in range(2):
                arrived(a2g.at[j, ox, zk(k), parts[half]], diag_ss.at[j, half, k], diag_rs.at[j, half, zk(k)])
        for half in range(2):
            @pl.loop(0, 2)
            def _(t):
                total = jnp.zeros((8 * rx, 256), F32)
                part = pl.ds(pl.multiple_of(t * 256, 256), 256)
                for zs in range(4):
                    lhs = a2g[j, :, zs].reshape(8 * rx, 1024)
                    rhs = eo[half, zs * 1024:(zs + 1) * 1024, part]
                    total = total + jnp.dot(lhs, rhs, preferred_element_type=F32)
                res = total.astype(BF16).reshape(2, 4, rx, 256)
                for xt in range(2):
                    ob[j, half, :, xt, :, part] = res[xt]

            for k in (2, 1, 3):
                send(ob.at[j, half, zk(k)], ow.at[j, half, z], ow_ss.at[j, half, k], ow_rs.at[j, half, z],
                     place(zk(k), xl, c, xh, y))

    def out_copy(j, half, k, xt):
        zs = zk(k)
        src = ow.at[j, half, zs, xt] if k else ob.at[j, half, z, xt]
        dst = out_ref.at[pl.ds(pl.multiple_of(j * rows + y * ry + xh * rx, rx), rx), pl.ds(half * 512, 512)]
        here = jnp.logical_and(xl == xt, jnp.logical_and(zs // 2 == xh, (zs % 2) * 2 + xl == y))
        copy = remote(src, dst, out_ss.at[j, half, k, xt], out_rs.at[j, half, m],
                      place(z, xt, c, zs // 2, (zs % 2) * 2 + xl))
        return here, copy, lambda: pltpu.make_async_copy(src, dst, out_rs.at[j, half, m]).start()

    def relay_out(j, half):
        for k in (0, 1, 3, 2):
            if k:
                arrived(ow.at[j, half, zk(k)], ow_ss.at[j, half, k], ow_rs.at[j, half, zk(k)])
            for xt in range(2):
                here, copy, own = out_copy(j, half, k, xt)
                pl.when(here)(own)
                pl.when(jnp.logical_not(here))(copy.start)

    def finish(j):
        for half in range(2):
            for ms in range(8):
                dst = out_ref.at[pl.ds(j * rows + (ms % 4) * ry + (ms // 4) * rx, rx), pl.ds(half * 512, 512)]
                arrived(dst, out_ss.at[j, 0, 0, 0], out_rs.at[j, half, ms])
            for k in range(4):
                for xt in range(2):
                    here, copy, own = out_copy(j, half, k, xt)
                    pl.when(jnp.logical_not(here))(copy.wait_send)
        for hr in range(2):
            cols = half_cols(xl if hr == 0 else ox)
            for k in range(1, 4):
                remote(p1.at[j, yk(k), :, :, cols], r1.at[j, hr, 3 - k], r1_ss.at[j, hr, k], r1_rs.at[j, hr, 3 - k],
                       place(z, xl, c, xh, yk(k))).wait_send()

    reduce_y(0, 0)
    relay_store(1, ox, xh)
    compute(1, zk(1), 0)
    compute(1, zk(3), 0)
    reduce_x(0, 0)
    send_partials(1, zk(1), 0)
    compute(1, zk(1), 1)
    compute(1, zk(3), 1)
    reduce_y(0, 1)
    attn_arrived(1, 2)
    compute(1, zk(2), 0)
    compute(1, zk(2), 1)
    reduce_x(0, 1)
    for hr in range(2):
        for k in (1, 3, 2):
            if k != 1 or hr != 0:
                send_partials(1, zk(k), hr)
    relay_store(2, xl, oh)
    send(eo.at[c], eo.at[c], eo_ss, eo_rs, place(z, xl, oc, xh, y))
    store_arrived()
    multiply_store(0)
    reduce_y(1, 0)
    reduce_y(1, 1)
    reduce_x(1, 0)
    reduce_z()
    reduce_x(1, 1)
    spread(0)
    relay_x(0)
    multiply_store(1)
    relay_z(0)
    arrived(eo.at[oc], eo_ss, eo_rs)
    multiply_out(0)
    reduce_zy()
    spread(1)
    relay_x(1)
    relay_z(1)
    relay_out(0, 0)
    relay_out(0, 1)
    multiply_out(1)
    relay_out(1, 0)
    relay_out(1, 1)
    for j in range(NCH):
        finish(j)
    for copy in sent:
        copy.wait_send()


def shards(old_store, block_map, expand_in, expand_out, attn, residual):
    tokens, width = attn.shape
    rows = tokens // NCH
    ry, rx = rows // 4, rows // 8
    dma = pltpu.SemaphoreType.DMA
    hbm = pl.BlockSpec(memory_space=pl.ANY)
    products = pl.pallas_call(
        chain_kernel,
        out_shape=jax.ShapeDtypeStruct((tokens, width), BF16),
        in_specs=[pl.BlockSpec(memory_space=pltpu.SMEM), hbm, hbm, hbm, hbm],
        out_specs=hbm,
        scratch_shapes=[
            pltpu.VMEM((4, tokens, width), BF16),
            pltpu.VMEM((4, 2, width, 128), BF16),
            pltpu.VMEM((4, 2, 512, 256), BF16),
            pltpu.VMEM((32, 512, BLOCK), BF16),
            pltpu.VMEM((2, 4096, 512), BF16),
            pltpu.VMEM((NCH, 4, 4, ry, 1024), BF16),
            pltpu.VMEM((NCH, 2, 3, 4, ry, 512), BF16),
            pltpu.VMEM((NCH, 2, 4, rx, 512), F32),
            pltpu.VMEM((NCH, 2, 4, rx, 512), BF16),
            pltpu.VMEM((NCH, 2, 4, rx, 512), BF16),
            pltpu.VMEM((NCH, 2, 4, 4 * rx, 512), BF16),
            pltpu.VMEM((NCH, 4, 4, 4 * rx, 256), BF16),
            pltpu.VMEM((3, 4, 4 * rx, 256), BF16),
            pltpu.VMEM((4, 4, 4 * rx, 256), BF16),
            pltpu.VMEM((4, 4 * rx, 256), BF16),
            pltpu.VMEM((NCH, 2, 4, 4 * rx, 1024), BF16),
            pltpu.VMEM((NCH, 2, 4, 2, rx, 512), BF16),
            pltpu.VMEM((NCH, 2, 4, 2, rx, 512), BF16),
            dma((5,)), dma((2, 3)), dma((4, 2)), dma((7,)), dma((4, 2)),
            dma((NCH, 4)), dma((NCH, 4)), dma, dma,
            dma((NCH, 2, 4)), dma((NCH, 2, 3)), dma((NCH, 2)), dma((NCH, 2)),
            dma((NCH, 2, 4)), dma((NCH, 2, 4)), dma((4,)), dma((3,)), dma((4, 4)), dma((4, 4)), dma((4,)), dma((4,)),
            dma((NCH, 2, 4)), dma((NCH, 2, 2, 4)), dma((NCH, 2, 4)), dma((NCH, 2, 4)),
            dma((NCH, 2, 4)), dma((NCH, 2, 4)), dma((NCH, 2, 4, 2)), dma((NCH, 2, 8)),
        ],
        compiler_params=pltpu.CompilerParams(
            collective_id=0, has_side_effects=True, vmem_limit_bytes=56 * 2**20
        ),
        name="chain",
    )(block_map, old_store, expand_in, expand_out, attn)
    return (products.astype(F32) + residual.astype(F32)).astype(BF16)


def solution(mesh):
    placed = (P("mp", "dp"), P(), P("mp", "dp"), P("dp", None), P("dp", "mp"), P("dp", "mp"))
    return jax.shard_map(
        shards, mesh=mesh, in_specs=placed, out_specs=P("dp", "mp"), check_vma=False
    )
```

```python
import jax
import jax.numpy as jnp
from jax import lax
from jax.experimental import pallas as pl
from jax.experimental.pallas import tpu as pltpu
from jax.sharding import PartitionSpec as P

MESH = pl.DeviceIdType.MESH
BLOCK = 128
NCH = 2
NEAR = 32
F32 = jnp.float32
BF16 = jnp.bfloat16


def place(z, xl, c, xh, y):
    return {"dp": z * 4 + xl * 2 + c, "mp": xh * 4 + y}


def dot_nt(a, b):
    return lax.dot_general(a, b, (((1,), (1,)), ((), ())), preferred_element_type=F32)


def chain_kernel(
    map_ref, store_ref, ein_ref, eout_ref, attn_ref, out_ref,
    attn_g, ein_g, s_g, eo_raw, eo, p1, r1, ysum, xs, xr, a1g, p2, r2, rm, q2, a2g, ob, ow,
    loc_sem, ein_ss, ein_rs, s_ss, s_rs, at_ss, at_rs, eo_ss, eo_rs, r1_ss, r1_rs, x_ss, x_rs,
    a1_ss, a1_rs, r2_ss, r2_rs, rm_ss, rm_rs, q2_ss, q2_rs, a2_ss, a2_rs, diag_ss, diag_rs, ow_ss, ow_rs, out_ss, out_rs,
):
    d = lax.axis_index("dp")
    m = lax.axis_index("mp")
    z, xl, c = d // 4, (d // 2) % 2, d % 2
    xh, y = m // 4, m % 4
    q0 = xl * 2 + c
    ox, oc, oh = 1 - xl, 1 - c, 1 - xh
    rows = attn_ref.shape[0] // NCH
    ry, rx = rows // 4, rows // 8
    sent = []

    def remote(src, dst, ss, rs, target):
        return pltpu.make_async_remote_copy(
            src_ref=src, dst_ref=dst, send_sem=ss, recv_sem=rs, device_id=target, device_id_type=MESH
        )

    def send(src, dst, ss, rs, target):
        copy = remote(src, dst, ss, rs, target)
        copy.start()
        sent.append(copy)

    def arrived(dst, ss, rs):
        remote(dst, dst, ss, rs, place(z, xl, oc, xh, y)).wait_recv()

    def zk(k):
        return lax.rem(z + k, 4)

    def yk(k):
        return lax.rem(y + k, 4)

    barrier = pltpu.get_barrier_semaphore()

    def greet(target):
        pl.semaphore_signal(barrier, inc=1, device_id=target, device_id_type=MESH)

    for k in (2, 1, 3):
        greet(place(zk(k), xl, c, xh, y))
        greet(place(z, xl, c, xh, yk(k)))
    greet(place(z, xl, c, oh, y))
    greet(place(z, ox, c, oh, y))
    greet(place(z, ox, c, xh, y))
    greet(place(z, xl, oc, xh, y))

    local = [
        pltpu.make_async_copy(attn_ref, attn_g.at[z], loc_sem.at[0]),
        pltpu.make_async_copy(ein_ref.at[:, :128], ein_g.at[q0, 0], loc_sem.at[1]),
        pltpu.make_async_copy(ein_ref.at[:, 128:], ein_g.at[q0, 1], loc_sem.at[4]),
        pltpu.make_async_copy(store_ref, s_g.at[q0, xh], loc_sem.at[2]),
    ]
    for copy in local:
        copy.start()

    pl.semaphore_wait(barrier, 10)

    for a in range(2):
        src = ein_ref.at[:, a * 128:(a + 1) * 128]
        send(src, ein_g.at[q0, a], ein_ss.at[a, 1], ein_rs.at[q0, a], place(z, ox, c, xh, y))
        send(src, ein_g.at[q0, a], ein_ss.at[a, 0], ein_rs.at[q0, a], place(z, xl, oc, xh, y))

    def attn_part(zs, j):
        return attn_g.at[zs, pl.ds(j * rows, rows)]

    def send_attn(j):
        for k in (1, 3):
            send(attn_ref.at[pl.ds(j * rows, rows)], attn_part(z, j), at_ss.at[j, k], at_rs.at[j, z],
                 place(zk(k), xl, c, xh, y))

    def attn_arrived(j, k):
        arrived(attn_part(zk(k), j), at_ss.at[j, k], at_rs.at[j, zk(k)])

    def attn_near(j):
        half = rows // 2
        for k in (1, 3):
            attn_arrived(j, 4 - k)
            src = attn_g.at[zk(4 - k), pl.ds(j * rows + (k // 2) * half, half)]
            send(src, src, at_ss.at[j, k - 1], at_rs.at[j, zk(4 - k)], place(zk(k), xl, c, xh, y))

    send_attn(0)

    mine = s_g.at[q0, xh]
    send(store_ref, mine, s_ss.at[0], s_rs.at[q0, xh], place(z, ox, c, oh, y))
    send(store_ref, mine, s_ss.at[1], s_rs.at[q0, xh], place(z, xl, oc, xh, y))

    @pl.loop(0, 32)
    def _(t):
        cols = pl.ds(pl.multiple_of(t * BLOCK, BLOCK), BLOCK)
        pltpu.make_async_copy(eout_ref.at[:, cols], eo_raw.at[t], loc_sem.at[3]).start()

    def half_cols(h):
        return pl.ds(pl.multiple_of(h * 512, 512), 512)

    def multiply_in(j, zs, hr, a):
        h = xl if hr == 0 else ox
        rhs = jnp.concatenate([ein_g[h * 2, a], ein_g[h * 2 + 1, a]], axis=1)
        res = jnp.dot(attn_g[zs, pl.ds(j * rows, rows), :], rhs, preferred_element_type=F32)
        res = res.astype(BF16).reshape(4, ry, 256)
        p1[j, :, zs, :, pl.ds(pl.multiple_of(h * 512 + a * 256, 256), 256)] = res

    def send_partials(j, zs, hr, first=0, width=512):
        cols = pl.ds(pl.multiple_of((xl if hr == 0 else ox) * 512 + first, 256), width)
        for k in (1, 3, 2):
            remote(p1.at[j, yk(k), zs, :, cols], r1.at[j, hr, 3 - k, zs, :, first:first + width],
                   r1_ss.at[j, hr, k], r1_rs.at[j, hr, 3 - k], place(z, xl, c, xh, yk(k))).start()

    def unit(j, zs, hr, a=None):
        if a is None:
            multiply_in(j, zs, hr, 0)
            multiply_in(j, zs, hr, 1)
            send_partials(j, zs, hr)
        else:
            multiply_in(j, zs, hr, a)
            send_partials(j, zs, hr, a * 256, 256)

    def compute(j, zs, hr):
        multiply_in(j, zs, hr, 0)
        multiply_in(j, zs, hr, 1)

    def ein_far(a):
        qa = ox * 2 + c
        arrived(ein_g.at[qa, a], ein_ss.at[a, 1], ein_rs.at[qa, a])
        send(ein_g.at[qa, a], ein_g.at[qa, a], ein_ss.at[a, 2], ein_rs.at[qa, a], place(z, xl, oc, xh, y))

    def ein_far_core(a):
        qb = ox * 2 + oc
        arrived(ein_g.at[qb, a], ein_ss.at[a, 2], ein_rs.at[qb, a])

    def send_store():
        send(store_ref, mine, s_ss.at[2], s_rs.at[q0, xh], place(z, ox, c, xh, y))

    def relay_store(i, xls, xhs):
        block = s_g.at[xls * 2 + c, xhs]
        arrived(block, s_ss.at[0], s_rs.at[xls * 2 + c, xhs])
        send(block, block, s_ss.at[3 + i], s_rs.at[xls * 2 + c, xhs], place(z, xl, oc, xh, y))
        if i == 1:
            send(block, block, s_ss.at[6], s_rs.at[xls * 2 + c, xhs], place(z, ox, c, oh, y))

    local[0].wait()
    local[1].wait()
    local[2].wait()
    for a in range(2):
        arrived(ein_g.at[xl * 2 + oc, a], ein_ss.at[a, 0], ein_rs.at[xl * 2 + oc, a])
    unit(0, z, 0)
    unit(1, z, 0)

    pltpu.make_async_copy(eo_raw, eo_raw, loc_sem.at[3]).wait()

    @pl.loop(0, 32)
    def _(t):
        zs, ys, b = t // 8, (t // 2) % 4, t % 2
        s = ((zs // 2) * 4 + ys) * 4 + (zs % 2) * 2 + b
        eo[c, pl.ds(pl.multiple_of(t * BLOCK, BLOCK), BLOCK), :] = eo_raw[map_ref[s]].T

    attn_near(0)
    send_attn(1)
    unit(0, zk(1), 0)
    unit(0, zk(3), 0)
    ein_far(0)
    ein_far_core(0)
    for k in (0, 1, 3):
        unit(0, zk(k), 1, 0)
    attn_arrived(0, 2)
    unit(0, zk(2), 0)
    unit(0, zk(2), 1, 0)
    ein_far(1)
    send_store()
    ein_far_core(1)
    for k in range(4):
        unit(0, zk(k), 1, 1)
    unit(1, z, 1)
    relay_store(0, ox, oh)
    attn_near(1)

    def store_arrived():
        local[3].wait()
        for xls in range(2):
            for xhs in range(2):
                qs = xls * 2 + oc
                arrived(s_g.at[qs, xhs], s_ss.at[0], s_rs.at[qs, xhs])

    def reduce_y(j, hr):
        h = xl if hr == 0 else ox
        cols = half_cols(h)
        for k in range(3):
            arrived(r1.at[j, hr, k], r1_ss.at[j, hr, 1], r1_rs.at[j, hr, k])

        @pl.loop(0, 4)
        def _(zs):
            total = p1[j, y, zs, :, cols].astype(F32)
            for k in range(3):
                total = total + r1[j, hr, k, zs].astype(F32)
            low, high = total[:rx], total[rx:]
            ysum[j, hr, zs] = jnp.where(xh == 0, low, high)
            xs[j, hr, zs] = jnp.where(xh == 0, high, low).astype(BF16)

        send(xs.at[j, hr], xr.at[j, hr], x_ss.at[j, hr], x_rs.at[j, hr], place(z, xl, c, oh, y))

    def reduce_x(j, hr):
        h = xl if hr == 0 else ox
        arrived(xr.at[j, hr], x_ss.at[j, hr], x_rs.at[j, hr])
        total = ysum[j, hr] + xr[j, hr].astype(F32)
        a1g[j, h, y] = total.astype(BF16).reshape(4 * rx, 512)
        for k in (2, 1, 3):
            send(a1g.at[j, h, y], a1g.at[j, h, y], a1_ss.at[j, hr, k], a1_rs.at[j, hr, y],
                 place(z, xl, c, xh, yk(k)))

    def multiply_store(j):
        for hr in range(2):
            h = xl if hr == 0 else ox
            for k in range(1, 4):
                arrived(a1g.at[j, h, yk(k)], a1_ss.at[j, hr, k], a1_rs.at[j, hr, yk(k)])

        for k in (2, 1, 3, 0):
            zt = zk(k)
            total = jnp.zeros((16 * rx, 256), F32)
            for q in range(4):
                first = (q % 2) * 128
                lhs = jnp.concatenate(
                    [a1g[j, q // 2, :, :, first:first + 128], a1g[j, q // 2, :, :, first + 256:first + 384]], axis=2
                ).reshape(16 * rx, 256)
                rhs = s_g[q, zt // 2, pl.ds(pl.multiple_of((zt % 2) * 256, 256), 256), :]
                total = total + dot_nt(lhs, rhs)
            p2[j, zt] = total.astype(BF16).reshape(4, 4 * rx, 256)
            if j == 0:
                if k:
                    send(p2.at[j, zt], r2.at[3 - k], r2_ss.at[k], r2_rs.at[3 - k], place(zt, xl, c, xh, y))
            else:
                for l in (2, 1, 3, 0):
                    if k or l:
                        send(p2.at[j, zt, yk(l)], rm.at[z, y], rm_ss.at[k, l], rm_rs.at[z, y],
                             place(zt, xl, c, xh, yk(l)))

    def a2_cols(ys):
        return pl.ds(pl.multiple_of(ys * 256, 256), 256)

    def reduce_z():
        for k in range(1, 4):
            arrived(r2.at[3 - k], r2_ss.at[k], r2_rs.at[3 - k])

        @pl.loop(0, 4)
        def _(yt):
            total = p2[0, z, yt].astype(F32)
            for k in range(3):
                total = total + r2[k, yt].astype(F32)
            q2[yt] = total.astype(BF16)

        for k in (2, 1, 3):
            send(q2.at[yk(k)], a2g.at[0, xl, z, :, a2_cols(y)], q2_ss.at[k], q2_rs.at[y], place(z, xl, c, xh, yk(k)))
        a2g[0, xl, z, :, a2_cols(y)] = q2[y]

    def reduce_zy():
        rm[z, y] = p2[1, z, y]
        for k in range(4):
            for l in range(4):
                if k or l:
                    arrived(rm.at[zk(k), yk(l)], rm_ss.at[k, l], rm_rs.at[zk(k), yk(l)])

        @pl.loop(0, 4)
        def _(ys):
            total = rm[0, ys].astype(F32)
            for zs in range(1, 4):
                total = total + rm[zs, ys].astype(F32)
            a2g[1, xl, z, :, a2_cols(ys)] = total.astype(BF16)

    def spread(j):
        if j == 0:
            for k in range(1, 4):
                arrived(a2g.at[j, xl, z, :, a2_cols(yk(k))], q2_ss.at[k], q2_rs.at[yk(k)])
        for half in (0, 1):
            to_x, to_z = a2g.at[j, xl, z, parts[half]], a2g.at[j, xl, z, parts[1 - half]]
            send(to_x, to_x, a2_ss.at[j, half, 0], a2_rs.at[j, half, xl, z], place(z, ox, c, xh, y))
            for k in (1, 3, 2):
                send(to_z, to_z, a2_ss.at[j, 1 - half, k], a2_rs.at[j, 1 - half, xl, z], place(zk(k), xl, c, xh, y))

    parts = (pl.ds(0, NEAR), pl.ds(NEAR, 4 * rx - NEAR))

    def block_arrived(j, half, xs_, k):
        arrived(a2g.at[j, xs_, zk(k), parts[half]], a2_ss.at[j, half, k], a2_rs.at[j, half, xs_, zk(k)])

    def relay_x(j):
        block_arrived(j, 0, ox, 0)
        for k in (1, 3, 2):
            half = a2g.at[j, ox, z, parts[0]]
            send(half, half, diag_ss.at[j, 0, k], diag_rs.at[j, 0, z], place(zk(k), xl, c, xh, y))

    def relay_z(j):
        for k in (1, 3, 2):
            block_arrived(j, 1, xl, k)
            half = a2g.at[j, xl, zk(k), parts[1]]
            send(half, half, diag_ss.at[j, 1, k], diag_rs.at[j, 1, zk(k)], place(z, ox, c, xh, y))

    def multiply_out(j):
        block_arrived(j, 1, ox, 0)
        for k in range(1, 4):
            block_arrived(j, 0, xl, k)
            for half in range(2):
                arrived(a2g.at[j, ox, zk(k), parts[half]], diag_ss.at[j, half, k], diag_rs.at[j, half, zk(k)])
        for half in range(2):
            @pl.loop(0, 2)
            def _(t):
                total = jnp.zeros((8 * rx, 256), F32)
                part = pl.ds(pl.multiple_of(t * 256, 256), 256)
                for zs in range(4):
                    lhs = a2g[j, :, zs].reshape(8 * rx, 1024)
                    rhs = eo[half, zs * 1024:(zs + 1) * 1024, part]
                    total = total + jnp.dot(lhs, rhs, preferred_element_type=F32)
                res = total.astype(BF16).reshape(2, 4, rx, 256)
                for xt in range(2):
                    ob[j, half, :, xt, :, part] = res[xt]

            for k in (2, 1, 3):
                send(ob.at[j, half, zk(k)], ow.at[j, half, z], ow_ss.at[j, half, k], ow_rs.at[j, half, z],
                     place(zk(k), xl, c, xh, y))

    def out_copy(j, half, k, xt):
        zs = zk(k)
        src = ow.at[j, half, zs, xt] if k else ob.at[j, half, z, xt]
        dst = out_ref.at[pl.ds(pl.multiple_of(j * rows + y * ry + xh * rx, rx), rx), pl.ds(half * 512, 512)]
        here = jnp.logical_and(xl == xt, jnp.logical_and(zs // 2 == xh, (zs % 2) * 2 + xl == y))
        copy = remote(src, dst, out_ss.at[j, half, k, xt], out_rs.at[j, half, m],
                      place(z, xt, c, zs // 2, (zs % 2) * 2 + xl))
        return here, copy, lambda: pltpu.make_async_copy(src, dst, out_rs.at[j, half, m]).start()

    def relay_out(j, half):
        for k in (0, 1, 3, 2):
            if k:
                arrived(ow.at[j, half, zk(k)], ow_ss.at[j, half, k], ow_rs.at[j, half, zk(k)])
            for xt in range(2):
                here, copy, own = out_copy(j, half, k, xt)
                pl.when(here)(own)
                pl.when(jnp.logical_not(here))(copy.start)

    def finish(j):
        for half in range(2):
            for ms in range(8):
                dst = out_ref.at[pl.ds(j * rows + (ms % 4) * ry + (ms // 4) * rx, rx), pl.ds(half * 512, 512)]
                arrived(dst, out_ss.at[j, 0, 0, 0], out_rs.at[j, half, ms])
            for k in range(4):
                for xt in range(2):
                    here, copy, own = out_copy(j, half, k, xt)
                    pl.when(jnp.logical_not(here))(copy.wait_send)
        for hr in range(2):
            cols = half_cols(xl if hr == 0 else ox)
            for k in range(1, 4):
                remote(p1.at[j, yk(k), :, :, cols], r1.at[j, hr, 3 - k], r1_ss.at[j, hr, k], r1_rs.at[j, hr, 3 - k],
                       place(z, xl, c, xh, yk(k))).wait_send()

    reduce_y(0, 0)
    relay_store(1, ox, xh)
    compute(1, zk(1), 0)
    compute(1, zk(3), 0)
    reduce_x(0, 0)
    send_partials(1, zk(1), 0)
    compute(1, zk(1), 1)
    compute(1, zk(3), 1)
    reduce_y(0, 1)
    attn_arrived(1, 2)
    compute(1, zk(2), 0)
    compute(1, zk(2), 1)
    reduce_x(0, 1)
    for hr in range(2):
        for k in (1, 3, 2):
            if k != 1 or hr != 0:
                send_partials(1, zk(k), hr)
    relay_store(2, xl, oh)
    store_arrived()
    multiply_store(0)
    send(eo.at[c], eo.at[c], eo_ss, eo_rs, place(z, xl, oc, xh, y))
    reduce_y(1, 0)
    reduce_y(1, 1)
    reduce_x(1, 0)
    reduce_z()
    reduce_x(1, 1)
    spread(0)
    relay_x(0)
    multiply_store(1)
    relay_z(0)
    arrived(eo.at[oc], eo_ss, eo_rs)
    multiply_out(0)
    reduce_zy()
    spread(1)
    relay_x(1)
    relay_z(1)
    relay_out(0, 0)
    relay_out(0, 1)
    multiply_out(1)
    relay_out(1, 0)
    relay_out(1, 1)
    for j in range(NCH):
        finish(j)
    for copy in sent:
        copy.wait_send()


def shards(old_store, block_map, expand_in, expand_out, attn, residual):
    tokens, width = attn.shape
    rows = tokens // NCH
    ry, rx = rows // 4, rows // 8
    dma = pltpu.SemaphoreType.DMA
    hbm = pl.BlockSpec(memory_space=pl.ANY)
    products = pl.pallas_call(
        chain_kernel,
        out_shape=jax.ShapeDtypeStruct((tokens, width), BF16),
        in_specs=[pl.BlockSpec(memory_space=pltpu.SMEM), hbm, hbm, hbm, hbm],
        out_specs=hbm,
        scratch_shapes=[
            pltpu.VMEM((4, tokens, width), BF16),
            pltpu.VMEM((4, 2, width, 128), BF16),
            pltpu.VMEM((4, 2, 512, 256), BF16),
            pltpu.VMEM((32, 512, BLOCK), BF16),
            pltpu.VMEM((2, 4096, 512), BF16),
            pltpu.VMEM((NCH, 4, 4, ry, 1024), BF16),
            pltpu.VMEM((NCH, 2, 3, 4, ry, 512), BF16),
            pltpu.VMEM((NCH, 2, 4, rx, 512), F32),
            pltpu.VMEM((NCH, 2, 4, rx, 512), BF16),
            pltpu.VMEM((NCH, 2, 4, rx, 512), BF16),
            pltpu.VMEM((NCH, 2, 4, 4 * rx, 512), BF16),
            pltpu.VMEM((NCH, 4, 4, 4 * rx, 256), BF16),
            pltpu.VMEM((3, 4, 4 * rx, 256), BF16),
            pltpu.VMEM((4, 4, 4 * rx, 256), BF16),
            pltpu.VMEM((4, 4 * rx, 256), BF16),
            pltpu.VMEM((NCH, 2, 4, 4 * rx, 1024), BF16),
            pltpu.VMEM((NCH, 2, 4, 2, rx, 512), BF16),
            pltpu.VMEM((NCH, 2, 4, 2, rx, 512), BF16),
            dma((5,)), dma((2, 3)), dma((4, 2)), dma((7,)), dma((4, 2)),
            dma((NCH, 4)), dma((NCH, 4)), dma, dma,
            dma((NCH, 2, 4)), dma((NCH, 2, 3)), dma((NCH, 2)), dma((NCH, 2)),
            dma((NCH, 2, 4)), dma((NCH, 2, 4)), dma((4,)), dma((3,)), dma((4, 4)), dma((4, 4)), dma((4,)), dma((4,)),
            dma((NCH, 2, 4)), dma((NCH, 2, 2, 4)), dma((NCH, 2, 4)), dma((NCH, 2, 4)),
            dma((NCH, 2, 4)), dma((NCH, 2, 4)), dma((NCH, 2, 4, 2)), dma((NCH, 2, 8)),
        ],
        compiler_params=pltpu.CompilerParams(
            collective_id=0, has_side_effects=True, vmem_limit_bytes=56 * 2**20
        ),
        name="chain",
    )(block_map, old_store, expand_in, expand_out, attn)
    return (products.astype(F32) + residual.astype(F32)).astype(BF16)


def solution(mesh):
    placed = (P("mp", "dp"), P(), P("mp", "dp"), P("dp", None), P("dp", "mp"), P("dp", "mp"))
    return jax.shard_map(
        shards, mesh=mesh, in_specs=placed, out_specs=P("dp", "mp"), check_vma=False
    )
```

```python
import jax
import jax.numpy as jnp
from jax import lax
from jax.experimental import pallas as pl
from jax.experimental.pallas import tpu as pltpu
from jax.sharding import PartitionSpec as P

MESH = pl.DeviceIdType.MESH
BLOCK = 128
NCH = 2
NEAR = 32
F32 = jnp.float32
BF16 = jnp.bfloat16


def place(z, xl, c, xh, y):
    return {"dp": z * 4 + xl * 2 + c, "mp": xh * 4 + y}


def dot_nt(a, b):
    return lax.dot_general(a, b, (((1,), (1,)), ((), ())), preferred_element_type=F32)


def chain_kernel(
    map_ref, store_ref, ein_ref, eout_ref, attn_ref, out_ref,
    attn_g, ein_g, s_g, eo_raw, eo, p1, r1, ysum, xs, xr, a1g, p2, r2, rm, q2, a2g, ob, ow,
    loc_sem, ein_ss, ein_rs, s_ss, s_rs, at_ss, at_rs, eo_ss, eo_rs, r1_ss, r1_rs, x_ss, x_rs,
    a1_ss, a1_rs, r2_ss, r2_rs, rm_ss, rm_rs, q2_ss, q2_rs, a2_ss, a2_rs, diag_ss, diag_rs, ow_ss, ow_rs, out_ss, out_rs,
):
    d = lax.axis_index("dp")
    m = lax.axis_index("mp")
    z, xl, c = d // 4, (d // 2) % 2, d % 2
    xh, y = m // 4, m % 4
    q0 = xl * 2 + c
    ox, oc, oh = 1 - xl, 1 - c, 1 - xh
    rows = attn_ref.shape[0] // NCH
    ry, rx = rows // 4, rows // 8
    sent = []

    def remote(src, dst, ss, rs, target):
        return pltpu.make_async_remote_copy(
            src_ref=src, dst_ref=dst, send_sem=ss, recv_sem=rs, device_id=target, device_id_type=MESH
        )

    def send(src, dst, ss, rs, target):
        copy = remote(src, dst, ss, rs, target)
        copy.start()
        sent.append(copy)

    def arrived(dst, ss, rs):
        remote(dst, dst, ss, rs, place(z, xl, oc, xh, y)).wait_recv()

    def zk(k):
        return lax.rem(z + k, 4)

    def yk(k):
        return lax.rem(y + k, 4)

    barrier = pltpu.get_barrier_semaphore()

    def greet(target):
        pl.semaphore_signal(barrier, inc=1, device_id=target, device_id_type=MESH)

    for k in (2, 1, 3):
        greet(place(z, xl, c, xh, yk(k)))
        if k != 2:
            greet(place(zk(k), xl, c, xh, y))
    greet(place(z, ox, c, oh, y))
    greet(place(z, ox, c, xh, y))
    greet(place(z, xl, oc, xh, y))

    local = [
        pltpu.make_async_copy(attn_ref, attn_g.at[z], loc_sem.at[0]),
        pltpu.make_async_copy(ein_ref.at[:, :128], ein_g.at[q0, 0], loc_sem.at[1]),
        pltpu.make_async_copy(ein_ref.at[:, 128:], ein_g.at[q0, 1], loc_sem.at[4]),
        pltpu.make_async_copy(store_ref, s_g.at[q0, xh], loc_sem.at[2]),
    ]
    for copy in local:
        copy.start()

    pl.semaphore_wait(barrier, 8)

    for a in range(2):
        src = ein_ref.at[:, a * 128:(a + 1) * 128]
        send(src, ein_g.at[q0, a], ein_ss.at[a, 1], ein_rs.at[q0, a], place(z, ox, c, xh, y))
        send(src, ein_g.at[q0, a], ein_ss.at[a, 0], ein_rs.at[q0, a], place(z, xl, oc, xh, y))

    def attn_part(zs, j):
        return attn_g.at[zs, pl.ds(j * rows, rows)]

    def send_attn(j):
        for k in (1, 3):
            send(attn_ref.at[pl.ds(j * rows, rows)], attn_part(z, j), at_ss.at[j, k], at_rs.at[j, z],
                 place(zk(k), xl, c, xh, y))

    def attn_arrived(j, k):
        arrived(attn_part(zk(k), j), at_ss.at[j, k], at_rs.at[j, zk(k)])

    def attn_near(j):
        half = rows // 2
        for k in (1, 3):
            attn_arrived(j, 4 - k)
            src = attn_g.at[zk(4 - k), pl.ds(j * rows + (k // 2) * half, half)]
            send(src, src, at_ss.at[j, k - 1], at_rs.at[j, zk(4 - k)], place(zk(k), xl, c, xh, y))

    send_attn(0)

    mine = s_g.at[q0, xh]
    send(store_ref, mine, s_ss.at[0], s_rs.at[q0, xh], place(z, ox, c, oh, y))
    send(store_ref, mine, s_ss.at[1], s_rs.at[q0, xh], place(z, xl, oc, xh, y))

    @pl.loop(0, 32)
    def _(t):
        cols = pl.ds(pl.multiple_of(t * BLOCK, BLOCK), BLOCK)
        pltpu.make_async_copy(eout_ref.at[:, cols], eo_raw.at[t], loc_sem.at[3]).start()

    def half_cols(h):
        return pl.ds(pl.multiple_of(h * 512, 512), 512)

    def multiply_in(j, zs, hr, a):
        h = xl if hr == 0 else ox
        rhs = jnp.concatenate([ein_g[h * 2, a], ein_g[h * 2 + 1, a]], axis=1)
        res = jnp.dot(attn_g[zs, pl.ds(j * rows, rows), :], rhs, preferred_element_type=F32)
        res = res.astype(BF16).reshape(4, ry, 256)
        p1[j, :, zs, :, pl.ds(pl.multiple_of(h * 512 + a * 256, 256), 256)] = res

    def send_partials(j, zs, hr, first=0, width=512):
        cols = pl.ds(pl.multiple_of((xl if hr == 0 else ox) * 512 + first, 256), width)
        for k in (1, 3, 2):
            remote(p1.at[j, yk(k), zs, :, cols], r1.at[j, hr, 3 - k, zs, :, first:first + width],
                   r1_ss.at[j, hr, k], r1_rs.at[j, hr, 3 - k], place(z, xl, c, xh, yk(k))).start()

    def unit(j, zs, hr, a=None):
        if a is None:
            multiply_in(j, zs, hr, 0)
            multiply_in(j, zs, hr, 1)
            send_partials(j, zs, hr)
        else:
            multiply_in(j, zs, hr, a)
            send_partials(j, zs, hr, a * 256, 256)

    def compute(j, zs, hr):
        multiply_in(j, zs, hr, 0)
        multiply_in(j, zs, hr, 1)

    def ein_far(a):
        qa = ox * 2 + c
        arrived(ein_g.at[qa, a], ein_ss.at[a, 1], ein_rs.at[qa, a])
        send(ein_g.at[qa, a], ein_g.at[qa, a], ein_ss.at[a, 2], ein_rs.at[qa, a], place(z, xl, oc, xh, y))

    def ein_far_core(a):
        qb = ox * 2 + oc
        arrived(ein_g.at[qb, a], ein_ss.at[a, 2], ein_rs.at[qb, a])

    def send_store():
        send(store_ref, mine, s_ss.at[2], s_rs.at[q0, xh], place(z, ox, c, xh, y))

    def relay_store(i, xls, xhs):
        block = s_g.at[xls * 2 + c, xhs]
        arrived(block, s_ss.at[0], s_rs.at[xls * 2 + c, xhs])
        send(block, block, s_ss.at[3 + i], s_rs.at[xls * 2 + c, xhs], place(z, xl, oc, xh, y))
        if i == 1:
            send(block, block, s_ss.at[6], s_rs.at[xls * 2 + c, xhs], place(z, ox, c, oh, y))

    local[0].wait()
    local[1].wait()
    local[2].wait()
    for a in range(2):
        arrived(ein_g.at[xl * 2 + oc, a], ein_ss.at[a, 0], ein_rs.at[xl * 2 + oc, a])
    unit(0, z, 0)
    unit(1, z, 0)

    pltpu.make_async_copy(eo_raw, eo_raw, loc_sem.at[3]).wait()

    @pl.loop(0, 32)
    def _(t):
        zs, ys, b = t // 8, (t // 2) % 4, t % 2
        s = ((zs // 2) * 4 + ys) * 4 + (zs % 2) * 2 + b
        eo[c, pl.ds(pl.multiple_of(t * BLOCK, BLOCK), BLOCK), :] = eo_raw[map_ref[s]].T

    attn_near(0)
    send_attn(1)
    unit(0, zk(1), 0)
    unit(0, zk(3), 0)
    ein_far(0)
    ein_far_core(0)
    for k in (0, 1, 3):
        unit(0, zk(k), 1, 0)
    attn_arrived(0, 2)
    unit(0, zk(2), 0)
    unit(0, zk(2), 1, 0)
    ein_far(1)
    send_store()
    ein_far_core(1)
    for k in range(4):
        unit(0, zk(k), 1, 1)
    unit(1, z, 1)
    relay_store(0, ox, oh)
    attn_near(1)

    def store_arrived():
        local[3].wait()
        for xls in range(2):
            for xhs in range(2):
                qs = xls * 2 + oc
                arrived(s_g.at[qs, xhs], s_ss.at[0], s_rs.at[qs, xhs])

    def reduce_y(j, hr):
        h = xl if hr == 0 else ox
        cols = half_cols(h)
        for k in range(3):
            arrived(r1.at[j, hr, k], r1_ss.at[j, hr, 1], r1_rs.at[j, hr, k])

        @pl.loop(0, 4)
        def _(zs):
            total = p1[j, y, zs, :, cols].astype(F32)
            for k in range(3):
                total = total + r1[j, hr, k, zs].astype(F32)
            low, high = total[:rx], total[rx:]
            ysum[j, hr, zs] = jnp.where(xh == 0, low, high)
            xs[j, hr, zs] = jnp.where(xh == 0, high, low).astype(BF16)

        send(xs.at[j, hr], xr.at[j, hr], x_ss.at[j, hr], x_rs.at[j, hr], place(z, xl, c, oh, y))

    def reduce_x(j, hr):
        h = xl if hr == 0 else ox
        arrived(xr.at[j, hr], x_ss.at[j, hr], x_rs.at[j, hr])
        total = ysum[j, hr] + xr[j, hr].astype(F32)
        a1g[j, h, y] = total.astype(BF16).reshape(4 * rx, 512)
        for k in (2, 1, 3):
            send(a1g.at[j, h, y], a1g.at[j, h, y], a1_ss.at[j, hr, k], a1_rs.at[j, hr, y],
                 place(z, xl, c, xh, yk(k)))

    def multiply_store(j):
        for hr in range(2):
            h = xl if hr == 0 else ox
            for k in range(1, 4):
                arrived(a1g.at[j, h, yk(k)], a1_ss.at[j, hr, k], a1_rs.at[j, hr, yk(k)])

        for k in (2, 1, 3, 0):
            zt = zk(k)
            total = jnp.zeros((16 * rx, 256), F32)
            for q in range(4):
                first = (q % 2) * 128
                lhs = jnp.concatenate(
                    [a1g[j, q // 2, :, :, first:first + 128], a1g[j, q // 2, :, :, first + 256:first + 384]], axis=2
                ).reshape(16 * rx, 256)
                rhs = s_g[q, zt // 2, pl.ds(pl.multiple_of((zt % 2) * 256, 256), 256), :]
                total = total + dot_nt(lhs, rhs)
            p2[j, zt] = total.astype(BF16).reshape(4, 4 * rx, 256)
            if j == 0:
                if k:
                    send(p2.at[j, zt], r2.at[3 - k], r2_ss.at[k], r2_rs.at[3 - k], place(zt, xl, c, xh, y))
            else:
                for l in (2, 1, 3, 0):
                    if k or l:
                        send(p2.at[j, zt, yk(l)], rm.at[z, y], rm_ss.at[k, l], rm_rs.at[z, y],
                             place(zt, xl, c, xh, yk(l)))

    def a2_cols(ys):
        return pl.ds(pl.multiple_of(ys * 256, 256), 256)

    def reduce_z():
        for k in range(1, 4):
            arrived(r2.at[3 - k], r2_ss.at[k], r2_rs.at[3 - k])

        @pl.loop(0, 4)
        def _(yt):
            total = p2[0, z, yt].astype(F32)
            for k in range(3):
                total = total + r2[k, yt].astype(F32)
            q2[yt] = total.astype(BF16)

        for k in (2, 1, 3):
            send(q2.at[yk(k)], a2g.at[0, xl, z, :, a2_cols(y)], q2_ss.at[k], q2_rs.at[y], place(z, xl, c, xh, yk(k)))
        a2g[0, xl, z, :, a2_cols(y)] = q2[y]

    def reduce_zy():
        rm[z, y] = p2[1, z, y]
        for k in range(4):
            for l in range(4):
                if k or l:
                    arrived(rm.at[zk(k), yk(l)], rm_ss.at[k, l], rm_rs.at[zk(k), yk(l)])

        @pl.loop(0, 4)
        def _(ys):
            total = rm[0, ys].astype(F32)
            for zs in range(1, 4):
                total = total + rm[zs, ys].astype(F32)
            a2g[1, xl, z, :, a2_cols(ys)] = total.astype(BF16)

    def spread(j):
        if j == 0:
            for k in range(1, 4):
                arrived(a2g.at[j, xl, z, :, a2_cols(yk(k))], q2_ss.at[k], q2_rs.at[yk(k)])
        for half in (0, 1):
            to_x, to_z = a2g.at[j, xl, z, parts[half]], a2g.at[j, xl, z, parts[1 - half]]
            send(to_x, to_x, a2_ss.at[j, half, 0], a2_rs.at[j, half, xl, z], place(z, ox, c, xh, y))
            for k in (1, 3, 2):
                send(to_z, to_z, a2_ss.at[j, 1 - half, k], a2_rs.at[j, 1 - half, xl, z], place(zk(k), xl, c, xh, y))

    parts = (pl.ds(0, NEAR), pl.ds(NEAR, 4 * rx - NEAR))

    def block_arrived(j, half, xs_, k):
        arrived(a2g.at[j, xs_, zk(k), parts[half]], a2_ss.at[j, half, k], a2_rs.at[j, half, xs_, zk(k)])

    def relay_x(j):
        block_arrived(j, 0, ox, 0)
        for k in (1, 3, 2):
            half = a2g.at[j, ox, z, parts[0]]
            send(half, half, diag_ss.at[j, 0, k], diag_rs.at[j, 0, z], place(zk(k), xl, c, xh, y))

    def relay_z(j):
        for k in (1, 3, 2):
            block_arrived(j, 1, xl, k)
            half = a2g.at[j, xl, zk(k), parts[1]]
            send(half, half, diag_ss.at[j, 1, k], diag_rs.at[j, 1, zk(k)], place(z, ox, c, xh, y))

    def multiply_out(j):
        block_arrived(j, 1, ox, 0)
        for k in range(1, 4):
            block_arrived(j, 0, xl, k)
            for half in range(2):
                arrived(a2g.at[j, ox, zk(k), parts[half]], diag_ss.at[j, half, k], diag_rs.at[j, half, zk(k)])
        for half in range(2):
            @pl.loop(0, 2)
            def _(t):
                total = jnp.zeros((8 * rx, 256), F32)
                part = pl.ds(pl.multiple_of(t * 256, 256), 256)
                for zs in range(4):
                    lhs = a2g[j, :, zs].reshape(8 * rx, 1024)
                    rhs = eo[half, zs * 1024:(zs + 1) * 1024, part]
                    total = total + jnp.dot(lhs, rhs, preferred_element_type=F32)
                res = total.astype(BF16).reshape(2, 4, rx, 256)
                for xt in range(2):
                    ob[j, half, :, xt, :, part] = res[xt]

            for k in (2, 1, 3):
                send(ob.at[j, half, zk(k)], ow.at[j, half, z], ow_ss.at[j, half, k], ow_rs.at[j, half, z],
                     place(zk(k), xl, c, xh, y))

    def out_copy(j, half, k, xt):
        zs = zk(k)
        src = ow.at[j, half, zs, xt] if k else ob.at[j, half, z, xt]
        dst = out_ref.at[pl.ds(pl.multiple_of(j * rows + y * ry + xh * rx, rx), rx), pl.ds(half * 512, 512)]
        here = jnp.logical_and(xl == xt, jnp.logical_and(zs // 2 == xh, (zs % 2) * 2 + xl == y))
        copy = remote(src, dst, out_ss.at[j, half, k, xt], out_rs.at[j, half, m],
                      place(z, xt, c, zs // 2, (zs % 2) * 2 + xl))
        return here, copy, lambda: pltpu.make_async_copy(src, dst, out_rs.at[j, half, m]).start()

    def relay_out(j, half):
        for k in (0, 1, 3, 2):
            if k:
                arrived(ow.at[j, half, zk(k)], ow_ss.at[j, half, k], ow_rs.at[j, half, zk(k)])
            for xt in range(2):
                here, copy, own = out_copy(j, half, k, xt)
                pl.when(here)(own)
                pl.when(jnp.logical_not(here))(copy.start)

    def finish(j):
        for half in range(2):
            for ms in range(8):
                dst = out_ref.at[pl.ds(j * rows + (ms % 4) * ry + (ms // 4) * rx, rx), pl.ds(half * 512, 512)]
                arrived(dst, out_ss.at[j, 0, 0, 0], out_rs.at[j, half, ms])
            for k in range(4):
                for xt in range(2):
                    here, copy, own = out_copy(j, half, k, xt)
                    pl.when(jnp.logical_not(here))(copy.wait_send)
        for hr in range(2):
            cols = half_cols(xl if hr == 0 else ox)
            for k in range(1, 4):
                remote(p1.at[j, yk(k), :, :, cols], r1.at[j, hr, 3 - k], r1_ss.at[j, hr, k], r1_rs.at[j, hr, 3 - k],
                       place(z, xl, c, xh, yk(k))).wait_send()

    reduce_y(0, 0)
    relay_store(1, ox, xh)
    compute(1, zk(1), 0)
    compute(1, zk(3), 0)
    reduce_x(0, 0)
    send_partials(1, zk(1), 0)
    compute(1, zk(1), 1)
    compute(1, zk(3), 1)
    reduce_y(0, 1)
    attn_arrived(1, 2)
    compute(1, zk(2), 0)
    compute(1, zk(2), 1)
    reduce_x(0, 1)
    for hr in range(2):
        for k in (1, 3, 2):
            if k != 1 or hr != 0:
                send_partials(1, zk(k), hr)
    relay_store(2, xl, oh)
    store_arrived()
    multiply_store(0)
    send(eo.at[c], eo.at[c], eo_ss, eo_rs, place(z, xl, oc, xh, y))
    reduce_y(1, 0)
    reduce_y(1, 1)
    reduce_x(1, 0)
    reduce_z()
    reduce_x(1, 1)
    spread(0)
    relay_x(0)
    multiply_store(1)
    relay_z(0)
    arrived(eo.at[oc], eo_ss, eo_rs)
    multiply_out(0)
    reduce_zy()
    spread(1)
    relay_x(1)
    relay_z(1)
    relay_out(0, 0)
    relay_out(0, 1)
    multiply_out(1)
    relay_out(1, 0)
    relay_out(1, 1)
    for j in range(NCH):
        finish(j)
    for copy in sent:
        copy.wait_send()


def shards(old_store, block_map, expand_in, expand_out, attn, residual):
    tokens, width = attn.shape
    rows = tokens // NCH
    ry, rx = rows // 4, rows // 8
    dma = pltpu.SemaphoreType.DMA
    hbm = pl.BlockSpec(memory_space=pl.ANY)
    products = pl.pallas_call(
        chain_kernel,
        out_shape=jax.ShapeDtypeStruct((tokens, width), BF16),
        in_specs=[pl.BlockSpec(memory_space=pltpu.SMEM), hbm, hbm, hbm, hbm],
        out_specs=hbm,
        scratch_shapes=[
            pltpu.VMEM((4, tokens, width), BF16),
            pltpu.VMEM((4, 2, width, 128), BF16),
            pltpu.VMEM((4, 2, 512, 256), BF16),
            pltpu.VMEM((32, 512, BLOCK), BF16),
            pltpu.VMEM((2, 4096, 512), BF16),
            pltpu.VMEM((NCH, 4, 4, ry, 1024), BF16),
            pltpu.VMEM((NCH, 2, 3, 4, ry, 512), BF16),
            pltpu.VMEM((NCH, 2, 4, rx, 512), F32),
            pltpu.VMEM((NCH, 2, 4, rx, 512), BF16),
            pltpu.VMEM((NCH, 2, 4, rx, 512), BF16),
            pltpu.VMEM((NCH, 2, 4, 4 * rx, 512), BF16),
            pltpu.VMEM((NCH, 4, 4, 4 * rx, 256), BF16),
            pltpu.VMEM((3, 4, 4 * rx, 256), BF16),
            pltpu.VMEM((4, 4, 4 * rx, 256), BF16),
            pltpu.VMEM((4, 4 * rx, 256), BF16),
            pltpu.VMEM((NCH, 2, 4, 4 * rx, 1024), BF16),
            pltpu.VMEM((NCH, 2, 4, 2, rx, 512), BF16),
            pltpu.VMEM((NCH, 2, 4, 2, rx, 512), BF16),
            dma((5,)), dma((2, 3)), dma((4, 2)), dma((7,)), dma((4, 2)),
            dma((NCH, 4)), dma((NCH, 4)), dma, dma,
            dma((NCH, 2, 4)), dma((NCH, 2, 3)), dma((NCH, 2)), dma((NCH, 2)),
            dma((NCH, 2, 4)), dma((NCH, 2, 4)), dma((4,)), dma((3,)), dma((4, 4)), dma((4, 4)), dma((4,)), dma((4,)),
            dma((NCH, 2, 4)), dma((NCH, 2, 2, 4)), dma((NCH, 2, 4)), dma((NCH, 2, 4)),
            dma((NCH, 2, 4)), dma((NCH, 2, 4)), dma((NCH, 2, 4, 2)), dma((NCH, 2, 8)),
        ],
        compiler_params=pltpu.CompilerParams(
            collective_id=0, has_side_effects=True, vmem_limit_bytes=56 * 2**20
        ),
        name="chain",
    )(block_map, old_store, expand_in, expand_out, attn)
    return (products.astype(F32) + residual.astype(F32)).astype(BF16)


def solution(mesh):
    placed = (P("mp", "dp"), P(), P("mp", "dp"), P("dp", None), P("dp", "mp"), P("dp", "mp"))
    return jax.shard_map(
        shards, mesh=mesh, in_specs=placed, out_specs=P("dp", "mp"), check_vma=False
    )
```
